128 devices in a mesh: chan: 8 (over y_hi, x), win: 4 (over z), freq: 4 (over y_lo, core).
Axes of the slice: x: 4, y: 4 (y_hi: 2, y_lo: 2; y = y_hi * 2 + y_lo), z: 4, core: 2. Of those that a mesh axis runs over, the one named last changes fastest.
Arguments:
- samples: bfloat16 [256, 512, 1024], P('win', 'chan', 'freq'), may hold values from -6 to 6
- partner: int32 [8, 8], replicated, may hold values from 0 to 7, as said below
Outputs:
- stacks: float32 [8, 8, 512, 64, 128], P('chan', None, 'freq', 'win')
The draws below stay inside these ranges and needn't reach their ends.
Inputs may be any that keep to these rules, and one draw needn't show every extreme that they name: Each row partner[r] is an involution of the blocks 0 .. 7. The rounds form 1 pass of 8 consecutive rounds; within each pass every unordered pair of different blocks is matched in exactly one round, and in one round every block is matched with itself.
All inputs are finite; a program needn't handle non-finite values.
Results may differ from the reference program's by a relative error of at most 0.0038.
Values may be sent and summed in bfloat16 or wider, within the bound.
A program may use at most 256 MiB of HBM per device.

```python
import math
import jax
import jax.numpy as jnp
from jax import lax

SEG = 1024
F = 512
H = 64
CH_DEV = 64
C = 512
SEGMENTS = 256
ROUNDS = 8
N_CHAN = 8


def draw_partner(key, part):
    key = jax.random.fold_in(key, 7)
    last = N_CHAN - 1
    rnd = jnp.arange(N_CHAN, dtype=jnp.int32)[:, None]
    player = jnp.arange(N_CHAN, dtype=jnp.int32)[None, :]
    circle = jnp.mod(2 * rnd - player + 4 * N_CHAN, max(last, 1))
    starting_position = jnp.where(player == last, rnd, jnp.where(player == rnd, last, circle))
    starting_position = jnp.where(rnd == last, jnp.broadcast_to(player, (N_CHAN, N_CHAN)), starting_position)

    def one_pass(pass_key):
        key_label, key_order = jax.random.split(pass_key)
        group_names = jax.random.permutation(key_label, N_CHAN).astype(jnp.int32)
        renamed_groups = jnp.zeros((N_CHAN, N_CHAN), jnp.int32).at[:, group_names].set(group_names[starting_position])
        ranking_permutation = jax.random.permutation(key_order, N_CHAN).astype(jnp.int32)
        return renamed_groups[ranking_permutation]
    pass_keys = jax.random.split(key, ROUNDS // N_CHAN)
    return jax.vmap(one_pass)(pass_keys).reshape(ROUNDS, N_CHAN).astype(jnp.int32)


def block_levels(stream_key, extent, cuts, smallest, top_value):
    def one(position, shards_of):
        heights = jax.random.uniform(jax.random.fold_in(jax.random.fold_in(stream_key, 6), position), (shards_of,), jnp.float32, smallest / len(cuts), top_value / len(cuts))
        return jnp.repeat(jnp.exp(heights), extent[position] // shards_of).reshape((-1,) + (1,) * (len(extent) - position - 1))

    factor_of = one(*cuts[0])
    for cut in cuts[1:]:
        factor_of = factor_of * one(*cut)
    return factor_of


def bell_draw(key, extent, spread, limit, cuts=(), kind=jnp.bfloat16):
    result = spread * jax.random.normal(key, extent, jnp.float32)
    if cuts:
        result = result * block_levels(key, extent, cuts, -0.22, 0.18)
    return jnp.clip(result, -limit, limit).astype(kind)


def setup_inputs(seed: int = 0) -> dict:
    seeds = jax.random.split(jax.random.key(seed), 3)
    samples = bell_draw(seeds[0], (SEGMENTS, C, SEG), 1.0, 6.0, ((0, 4), (1, 8), (2, 4)))
    partner = draw_partner(jax.random.fold_in(seeds[2], 71), 0)
    return dict(samples=samples, partner=partner)


def make_tables():
    n = jnp.arange(SEG, dtype=jnp.int32)[:, None]
    f = jnp.arange(F, dtype=jnp.int32)[None, :]
    phase = (n * f % SEG).astype(jnp.float32)
    angle = phase * (2.0 * math.pi / SEG)
    norm = 1.0 / math.sqrt(SEG)
    return ((jnp.cos(angle) * norm).astype(jnp.bfloat16), (-jnp.sin(angle) * norm).astype(jnp.bfloat16))

def reference(samples, partner):
    table_cos, table_sin = make_tables()
    flat = samples.reshape(SEGMENTS * C, SEG)
    fourier_inphase = jnp.dot(flat, table_cos, preferred_element_type=jnp.float32)
    spec_im = jnp.dot(flat, table_sin, preferred_element_type=jnp.float32)
    power = fourier_inphase * fourier_inphase + spec_im * spec_im
    padded = jnp.pad(power, ((0, 0), (H, H)))
    summed = lax.reduce_window(padded, jnp.float32(0.0), lax.add, (1, 2 * H + 1), (1, 1), 'VALID')
    smooth = summed / (2 * H + 1)
    scale = lax.rsqrt(smooth + 1e-06)
    white_re = (fourier_inphase * scale).astype(jnp.bfloat16).reshape(SEGMENTS, C, F).transpose(2, 0, 1)
    white_im = (spec_im * scale).astype(jnp.bfloat16).reshape(SEGMENTS, C, F).transpose(2, 0, 1)
    blocks = []
    for block in range(N_CHAN):
        lo = block * CH_DEV
        blocks.append(jnp.concatenate([white_re[:, :, lo:lo + CH_DEV], white_im[:, :, lo:lo + CH_DEV]], axis=2))
    blocks = jnp.stack(blocks, 0)
    rows = []
    for block in range(N_CHAN):
        mine = blocks[block].astype(jnp.float32)
        per_round = []
        for step in range(ROUNDS):
            other = lax.dynamic_index_in_dim(blocks, partner[step, block].astype(jnp.int32), 0, keepdims=False).astype(jnp.float32)
            prod = jnp.einsum('fkc,fkd->fcd', mine, other)
            inphase_share = prod[:, :CH_DEV, :CH_DEV] + prod[:, CH_DEV:, CH_DEV:]
            imaginary_component = prod[:, :CH_DEV, CH_DEV:] - prod[:, CH_DEV:, :CH_DEV]
            per_round.append(jnp.concatenate([inphase_share, imaginary_component], axis=2) * (1.0 / SEGMENTS))
        rows.append(jnp.stack(per_round, 0))
    return jnp.stack(rows, 0)
```

```python
import functools
import math

import jax
import jax.numpy as jnp
import ml_dtypes
import numpy as np
from jax import lax
from jax.experimental import pallas as pl
from jax.experimental.pallas import tpu as pltpu
from jax.sharding import PartitionSpec as P

MESH = pl.DeviceIdType.MESH
NT = (((1,), (1,)), ((), ()))

LENGTH = 1024
BINS = 512
MARGIN = 64
SEGS = 64
SEGMENTS = 256
BLOCK = 64
CHANS = 512
ROWS = 1024


def tables():
    n = np.arange(LENGTH)[None, :]
    f = np.arange(BINS)[:, None]
    angle = (n * f % LENGTH) * (2.0 * math.pi / LENGTH)
    both = np.concatenate([np.cos(angle), -np.sin(angle)], axis=0) / math.sqrt(LENGTH)
    return both.astype(np.float32).astype(ml_dtypes.bfloat16)


def position():
    chan, win, freq = (lax.axis_index(name) for name in ("chan", "win", "freq"))
    return chan // 4, chan % 4, win, freq // 2, freq % 2


def peer_all(i, s):
    y_hi, x, z, y_lo, core = position()
    y = (y_hi * 2 + y_lo + i // 2 % 2 + 2 * s) % 4
    return (
        (y // 2) * 4 + (x + i // 4 % 4 + 2 * s) % 4,
        (z + i // 16 + 2 * s) % 4,
        y % 2 * 2 + (core + i % 2) % 2,
    )


def peer_rows(i, s):
    y_hi, x, z, y_lo, core = position()
    return (
        (y_hi + s) % 2 * 4 + (x + i % 4 + 2 * s) % 4,
        (z + i // 4 + 2 * s) % 4,
        y_lo * 2 + core,
    )


def each_peer(half, peer, act):
    act(peer(0, 1))

    def body(i, carry):
        act(peer(i, 0))
        act(peer(i, 1))
        return carry

    lax.fori_loop(1, half, body, 0)


def main_kernel(
    x_ref, table_ref, out_ref,
    table, got, wide, rows, spec, high, low, mixed, white, a_mat, b_mat, sums,
    table_sem, send1, recv1, send3, recv3, send5, recv5,
):
    chan, win, freq = (lax.axis_index(name) for name in ("chan", "win", "freq"))
    holder = chan * 4 + win
    piece = x_ref.shape[2]
    take_table = pltpu.make_async_copy(table_ref, table, table_sem)
    take_table.start()

    barrier = pltpu.get_barrier_semaphore()
    each_peer(64, peer_all, lambda d: pl.semaphore_signal(
        barrier, inc=1, device_id=d, device_id_type=MESH))
    pl.semaphore_wait(barrier, 127)

    here = pl.ds(pl.multiple_of(freq * piece, piece), piece)
    for step in (2, 3, 1):
        k = (freq + step) % 4
        pltpu.make_async_remote_copy(
            src_ref=x_ref.at[:, pl.ds(pl.multiple_of(k * 16, 16), 16), :],
            dst_ref=got.at[:, :, here],
            send_sem=send1, recv_sem=recv1,
            device_id=(chan, win, k), device_id_type=MESH,
        ).start()
    pltpu.make_async_copy(
        x_ref.at[:, pl.ds(pl.multiple_of(freq * 16, 16), 16), :], got.at[:, :, here], recv1
    ).start()
    pltpu.make_async_copy(got, got, recv1).wait()

    def reorder(c, carry):
        at = pl.ds(pl.multiple_of(c * 128, 128), 128)
        wide[...] = got[:, :, at].astype(jnp.float32).reshape(ROWS, 128)
        for ch in range(16):
            rows[ch * 64:(ch + 1) * 64, at] = wide[pl.ds(ch, 64, stride=16), :].astype(jnp.bfloat16)
        return carry

    lax.fori_loop(0, LENGTH // 128, reorder, 0)
    take_table.wait()

    def transform(t, carry):
        at = pl.ds(pl.multiple_of(t * 128, 128), 128)
        spec[at, :] = lax.dot_general(
            table[at, :], rows[...], NT, preferred_element_type=jnp.float32)
        return carry

    lax.fori_loop(0, 2 * BINS // 128, transform, 0)

    def powers(t, carry):
        at = pl.ds(pl.multiple_of(t * 32, 32), 32)
        im_at = pl.ds(pl.multiple_of(BINS + t * 32, 32), 32)
        re, im = spec[at, :], spec[im_at, :]
        power = re * re + im * im
        top = power.astype(jnp.bfloat16)
        high[at, :] = top
        low[at, :] = (power - top.astype(jnp.float32)).astype(jnp.bfloat16)
        return carry

    lax.fori_loop(0, BINS // 32, powers, 0)

    left = lax.broadcasted_iota(jnp.int32, (128, 128), 1) < 64

    def whiten(t, carry):
        first = t * 128
        start = jnp.clip(first - 64, 0, BINS - 256)
        window = pl.ds(pl.multiple_of(start, 64), 256)
        apart = (lax.broadcasted_iota(jnp.int32, (128, 256), 1) + start) - (
            lax.broadcasted_iota(jnp.int32, (128, 256), 0) + first)
        band = jnp.where((apart >= -MARGIN) & (apart <= MARGIN), 1.0, 0.0).astype(jnp.bfloat16)
        smooth = (
            jnp.dot(band, high[window, :], preferred_element_type=jnp.float32)
            + jnp.dot(band, low[window, :], preferred_element_type=jnp.float32)
        ) / (2 * MARGIN + 1)
        scale = lax.rsqrt(smooth + 1e-06)
        re = spec[pl.ds(pl.multiple_of(first, 128), 128), :] * scale
        im = spec[pl.ds(pl.multiple_of(BINS + first, 128), 128), :] * scale
        for c in range(8):
            a, b = re[:, c * 128:(c + 1) * 128], im[:, c * 128:(c + 1) * 128]
            mixed[pl.ds(2 * c, 128, stride=16), :] = jnp.where(left, a, pltpu.roll(b, 64, 1))
            mixed[pl.ds(2 * c + 1, 128, stride=16), :] = jnp.where(left, pltpu.roll(a, 64, 1), b)
        white[pl.ds(pl.multiple_of(first, 128), 128)] = (
            mixed[...].reshape(128, 16, 128).astype(jnp.bfloat16))
        return carry

    lax.fori_loop(0, BINS // 128, whiten, 0)

    place_ch = pl.ds(pl.multiple_of(chan * 64 + freq * 16, 16), 16)
    place_k = pl.ds(pl.multiple_of(win * 128, 128), 128)

    def send_white(d):
        pltpu.make_async_remote_copy(
            src_ref=white.at[pl.ds(d[2] * 128 + (d[0] * 4 + d[1]) * 4, 4)],
            dst_ref=a_mat.at[:, place_ch, place_k],
            send_sem=send3, recv_sem=recv3, device_id=d, device_id_type=MESH,
        ).start()

    each_peer(64, peer_all, send_white)
    pltpu.make_async_copy(
        white.at[pl.ds(freq * 128 + holder * 4, 4)], a_mat.at[:, place_ch, place_k], recv3
    ).start()
    pltpu.make_async_copy(a_mat, a_mat, recv3).wait()

    sign = jnp.where(lax.broadcasted_iota(jnp.int32, (64, 128), 1) < 64, 1.0, -1.0)

    def cross(b, carry):
        def turn(q, c):
            block = a_mat[b, pl.ds(pl.multiple_of(q * 64, 64), 64), :]
            b_mat[pl.ds(pl.multiple_of(q * 128, 128), 64), :] = block
            for w in range(4):
                part = block[:, w * 128:(w + 1) * 128].astype(jnp.float32)
                b_mat[pl.ds(pl.multiple_of(q * 128 + 64, 64), 64), w * 128:(w + 1) * 128] = (
                    pltpu.roll(part, 64, 1) * sign).astype(jnp.bfloat16)
            return c

        lax.fori_loop(0, 8, turn, 0)

        def multiply(m, c):
            tile = lax.dot_general(
                a_mat[b, pl.ds(pl.multiple_of(m * 128, 128), 128), :], b_mat[...], NT,
                preferred_element_type=jnp.float32)
            tile = (tile * (1.0 / SEGMENTS)).astype(jnp.bfloat16)
            for q in range(8):
                sums[pl.ds(m * 8, 8), b, q] = tile[:, q * 128:(q + 1) * 128].reshape(8, 16, 128)
            return c

        lax.fori_loop(0, 4, multiply, 0)

        def send_sums(d):
            pltpu.make_async_remote_copy(
                src_ref=sums.at[d[0] * 4 + d[1], b],
                dst_ref=out_ref.at[holder * 4 + b],
                send_sem=send5, recv_sem=recv5, device_id=d, device_id_type=MESH,
            ).start()

        each_peer(16, peer_rows, send_sums)
        pltpu.make_async_copy(sums.at[holder, b], out_ref.at[holder * 4 + b], recv5).start()
        return carry

    lax.fori_loop(0, 4, cross, 0)

    pltpu.make_async_copy(out_ref, out_ref, recv5).wait()
    three = pl.ds(0, 48)
    pltpu.make_async_copy(got.at[pl.ds(0, 48)], got.at[pl.ds(0, 48)], send1).wait()
    pltpu.make_async_copy(white.at[pl.ds(0, 508)], white.at[pl.ds(0, 508)], send3).wait()
    pltpu.make_async_copy(sums.at[pl.ds(0, 31)], sums.at[pl.ds(0, 31)], send5).wait()


def order_kernel(partner_ref, in_ref, out_ref):
    chan = lax.axis_index("chan")
    for r in range(8):
        out_ref[0, r] = in_ref[:, partner_ref[r, chan]].astype(jnp.float32)


def per_device(samples, partner):
    table = jnp.asarray(tables())
    sums = pl.pallas_call(
        main_kernel,
        out_shape=jax.ShapeDtypeStruct((128, 8, 16, 128), jnp.bfloat16),
        in_specs=[pl.BlockSpec(memory_space=pl.ANY)] * 2,
        out_specs=pl.BlockSpec(memory_space=pl.ANY),
        scratch_shapes=[
            pltpu.VMEM((2 * BINS, LENGTH), jnp.bfloat16),
            pltpu.VMEM((SEGS, 16, LENGTH), jnp.bfloat16),
            pltpu.VMEM((ROWS, 128), jnp.float32),
            pltpu.VMEM((ROWS, LENGTH), jnp.bfloat16),
            pltpu.VMEM((2 * BINS, ROWS), jnp.float32),
            pltpu.VMEM((BINS, ROWS), jnp.bfloat16),
            pltpu.VMEM((BINS, ROWS), jnp.bfloat16),
            pltpu.VMEM((128 * 16, 128), jnp.float32),
            pltpu.VMEM((BINS, 16, 128), jnp.bfloat16),
            pltpu.VMEM((4, CHANS, 512), jnp.bfloat16),
            pltpu.VMEM((2 * CHANS, 512), jnp.bfloat16),
            pltpu.VMEM((32, 4, 8, 16, 128), jnp.bfloat16),
        ] + [pltpu.SemaphoreType.DMA] * 7,
        compiler_params=pltpu.CompilerParams(
            collective_id=0, has_side_effects=True, vmem_limit_bytes=48 * 2**20),
        name="spectra",
    )(samples, table)
    chunk = 16
    return pl.pallas_call(
        order_kernel,
        out_shape=jax.ShapeDtypeStruct((1, 8, 128, 16, 128), jnp.float32),
        grid_spec=pltpu.PrefetchScalarGridSpec(
            num_scalar_prefetch=1,
            grid=(128 // chunk,),
            in_specs=[pl.BlockSpec((chunk, 8, 16, 128), lambda i, part: (i, 0, 0, 0))],
            out_specs=pl.BlockSpec((1, 8, chunk, 16, 128), lambda i, part: (0, 0, i, 0, 0)),
        ),
        compiler_params=pltpu.CompilerParams(vmem_limit_bytes=16 * 2**20),
        name="order",
    )(partner, sums)


def solution(mesh):
    in_specs = (P("win", "chan", "freq"), P())
    out_specs = P("chan", None, "freq", "win", None)
    return jax.shard_map(
        per_device, mesh=mesh, in_specs=in_specs, out_specs=out_specs, check_vma=False
    )
```

```python
import functools
import math

import jax
import jax.numpy as jnp
import ml_dtypes
import numpy as np
from jax import lax
from jax.experimental import pallas as pl
from jax.experimental.pallas import tpu as pltpu
from jax.sharding import PartitionSpec as P

MESH = pl.DeviceIdType.MESH
NT = (((1,), (1,)), ((), ()))

LENGTH = 1024
BINS = 512
MARGIN = 64
SEGS = 64
SEGMENTS = 256
BLOCK = 64
CHANS = 512
ROWS = 1024


def tables():
    n = np.arange(LENGTH)[None, :]
    f = np.arange(BINS)[:, None]
    angle = (n * f % LENGTH) * (2.0 * math.pi / LENGTH)
    both = np.concatenate([np.cos(angle), -np.sin(angle)], axis=0) / math.sqrt(LENGTH)
    return both.astype(np.float32).astype(ml_dtypes.bfloat16)


def position():
    chan, win, freq = (lax.axis_index(name) for name in ("chan", "win", "freq"))
    return chan // 4, chan % 4, win, freq // 2, freq % 2


def peer_all(i, s):
    y_hi, x, z, y_lo, core = position()
    y = (y_hi * 2 + y_lo + i // 2 % 2 + 2 * s) % 4
    return (
        (y // 2) * 4 + (x + i // 4 % 4 + 2 * s) % 4,
        (z + i // 16 + 2 * s) % 4,
        y % 2 * 2 + (core + i % 2) % 2,
    )


def peer_rows(i, s):
    y_hi, x, z, y_lo, core = position()
    return (
        (y_hi + s) % 2 * 4 + (x + i % 4 + 2 * s) % 4,
        (z + i // 4 + 2 * s) % 4,
        y_lo * 2 + core,
    )


def peer_share(k, i, s):
    y_hi, x, z, y_lo, core = position()
    y = (y_hi * 2 + (y_lo * 2 + core + k) % 4 // 2 + 2 * s) % 4
    return (
        y // 2 * 4 + (x + i % 4 + 2 * s) % 4,
        (z + i // 4 + 2 * s) % 4,
        (y_lo * 2 + core + k) % 4,
    )


def each_peer(half, peer, act, skip_own=True):
    if skip_own is not True:

        @pl.when(jnp.logical_not(skip_own))
        def _():
            act(peer(0, 0))

    act(peer(0, 1))

    def body(i, carry):
        act(peer(i, 0))
        act(peer(i, 1))
        return carry

    lax.fori_loop(1, half, body, 0)


def main_kernel(
    x_ref, table_ref, out_ref,
    table, got, wide, rows, spec, high, low, mixed, white, a_mat, b_mat, sums,
    table_sem, send1, recv1, send3, recv3, send5, recv5, in_sem,
):
    chan, win, freq = (lax.axis_index(name) for name in ("chan", "win", "freq"))
    holder = chan * 4 + win
    piece = x_ref.shape[2]
    take_table = pltpu.make_async_copy(table_ref, table, table_sem)
    take_table.start()

    barrier = pltpu.get_barrier_semaphore()
    y_hi, x, z, y_lo, core = position()
    along_x = [(y_hi * 4 + (x + i) % 4, win, freq) for i in (1, 2, 3)]
    along_z = [(chan, (z + i) % 4, freq) for i in (1, 2, 3)]
    along_freq = [(chan, win, (freq + i) % 4) for i in (1, 2, 3)]

    def tell(semaphore, devices):
        for d in devices:
            pl.semaphore_signal(semaphore, inc=1, device_id=d, device_id_type=MESH)

    tell(barrier, along_freq + along_x + along_z + [((1 - y_hi) * 4 + x, win, freq)])
    pl.semaphore_wait(barrier, 10)

    def across(i):
        return (y_lo + i // 2) % 2 * 2 + (core + i % 2) % 2

    def stretch(k, size=1):
        return pl.ds(pl.multiple_of(k * piece, size * piece), size * piece)

    pltpu.make_async_copy(
        x_ref.at[:, pl.ds(pl.multiple_of(freq * 16, 16), 16), :],
        got.at[:, :, stretch(freq)], recv1.at[0],
    ).start()
    for i in (2, 1, 3):
        k = across(i)
        pltpu.make_async_remote_copy(
            src_ref=x_ref.at[:, pl.ds(pl.multiple_of(k * 16, 16), 16), :],
            dst_ref=got.at[:, :, stretch(freq)],
            send_sem=send1, recv_sem=recv1.at[i],
            device_id=(chan, win, k), device_id_type=MESH,
        ).start()

    def arrived(i):
        part = got.at[:, :, stretch(across(i))]
        pltpu.make_async_copy(part, part, recv1.at[i]).wait()

    def reorder(k):
        def body(c, carry):
            at = pl.ds(pl.multiple_of(k * piece + c * 128, 128), 128)
            wide[...] = got[:, :, at].astype(jnp.float32).reshape(ROWS, 128)
            for ch in range(16):
                rows[ch * 64:(ch + 1) * 64, at] = (
                    wide[pl.ds(ch, 64, stride=16), :].astype(jnp.bfloat16))
            return carry

        lax.fori_loop(0, piece // 128, body, 0)

    def transform(k, size, first):
        span = stretch(k, size)

        def body(t, carry):
            at = pl.ds(pl.multiple_of(t * 256, 256), 256)
            term = lax.dot_general(
                table[:, span], rows[at, span], NT, preferred_element_type=jnp.float32)
            spec[:, at] = term if first else spec[:, at] + term
            return carry

        lax.fori_loop(0, ROWS // 256, body, 0)

    tell(in_sem.at[0], along_z)
    take_table.wait()
    for i in (0, 1):
        arrived(i)
        reorder(across(i))
    pl.semaphore_wait(in_sem.at[0], 3)
    tell(in_sem.at[1], along_x)
    transform(y_lo * 2, 2, True)
    pl.semaphore_wait(in_sem.at[1], 3)
    tell(in_sem.at[2], along_freq)
    for i in (2, 3):
        arrived(i)
        reorder(across(i))
        transform(across(i), 1, False)

    def powers(t, carry):
        at = pl.ds(pl.multiple_of(t * 32, 32), 32)
        im_at = pl.ds(pl.multiple_of(BINS + t * 32, 32), 32)
        re, im = spec[at, :], spec[im_at, :]
        power = re * re + im * im
        top = power.astype(jnp.bfloat16)
        high[at, :] = top
        low[at, :] = (power - top.astype(jnp.float32)).astype(jnp.bfloat16)
        return carry

    lax.fori_loop(0, BINS // 32, powers, 0)

    place_ch = pl.ds(pl.multiple_of(chan * 64 + freq * 16, 16), 16)
    place_k = pl.ds(pl.multiple_of(win * 128, 128), 128)

    def white_of(d, h):
        return white.at[pl.ds(d[2] * 128 + (d[0] * 4 + d[1]) * 4 + 2 * h, 2)]

    def send_white(h, d):
        pltpu.make_async_remote_copy(
            src_ref=white_of(d, h),
            dst_ref=a_mat.at[pl.ds(2 * h, 2), place_ch, place_k],
            send_sem=send3, recv_sem=recv3.at[h], device_id=d, device_id_type=MESH,
        ).start()

    def send_share(i, h):
        each_peer(
            16, functools.partial(peer_share, i), functools.partial(send_white, h), i == 0)

    left = lax.broadcasted_iota(jnp.int32, (128, 128), 1) < 64

    def whiten(i, carry):
        t = (freq + i) % 4
        first = t * 128
        start = jnp.clip(first - 64, 0, BINS - 256)
        window = pl.ds(pl.multiple_of(start, 64), 256)
        apart = (lax.broadcasted_iota(jnp.int32, (128, 256), 1) + start) - (
            lax.broadcasted_iota(jnp.int32, (128, 256), 0) + first)
        band = jnp.where((apart >= -MARGIN) & (apart <= MARGIN), 1.0, 0.0).astype(jnp.bfloat16)
        smooth = (
            jnp.dot(band, high[window, :], preferred_element_type=jnp.float32)
            + jnp.dot(band, low[window, :], preferred_element_type=jnp.float32)
        ) / (2 * MARGIN + 1)
        scale = lax.rsqrt(smooth + 1e-06)
        re = spec[pl.ds(pl.multiple_of(first, 128), 128), :] * scale
        im = spec[pl.ds(pl.multiple_of(BINS + first, 128), 128), :] * scale
        for c in range(8):
            a, b = re[:, c * 128:(c + 1) * 128], im[:, c * 128:(c + 1) * 128]
            mixed[pl.ds(2 * c, 128, stride=16), :] = jnp.where(left, a, pltpu.roll(b, 64, 1))
            mixed[pl.ds(2 * c + 1, 128, stride=16), :] = jnp.where(left, pltpu.roll(a, 64, 1), b)
        white[pl.ds(pl.multiple_of(first, 128), 128)] = (
            mixed[...].reshape(128, 16, 128).astype(jnp.bfloat16))
        send_share(i, 0)
        return carry

    pl.semaphore_wait(in_sem.at[2], 3)
    lax.fori_loop(0, BINS // 128, whiten, 0)
    for h in range(2):
        pltpu.make_async_copy(
            white_of((chan, win, freq), h), a_mat.at[pl.ds(2 * h, 2), place_ch, place_k],
            recv3.at[h],
        ).start()

    def send_rest(i, carry):
        send_share(i, 1)
        return carry

    lax.fori_loop(0, 4, send_rest, 0)

    sign = jnp.where(lax.broadcasted_iota(jnp.int32, (64, 128), 1) < 64, 1.0, -1.0)

    def cross(b, carry):
        def multiply(m, c):
            for h in range(2):
                block = a_mat[b, pl.ds(pl.multiple_of(m * 128 + h * 64, 64), 64), :]
                b_mat[h * 128:h * 128 + 64, :] = block
                for w in range(4):
                    part = block[:, w * 128:(w + 1) * 128].astype(jnp.float32)
                    b_mat[h * 128 + 64:h * 128 + 128, w * 128:(w + 1) * 128] = (
                        pltpu.roll(part, 64, 1) * sign).astype(jnp.bfloat16)
            tile = lax.dot_general(
                a_mat[b], b_mat[...], NT, preferred_element_type=jnp.float32)
            tile = (tile * (1.0 / SEGMENTS)).astype(jnp.bfloat16)
            for h in range(2):
                sums[:, b, m * 2 + h] = tile[:, h * 128:(h + 1) * 128].reshape(32, 16, 128)
            return c

        lax.fori_loop(0, 4, multiply, 0)

        def send_sums(d):
            pltpu.make_async_remote_copy(
                src_ref=sums.at[d[0] * 4 + d[1], b],
                dst_ref=out_ref.at[holder * 4 + b],
                send_sem=send5, recv_sem=recv5, device_id=d, device_id_type=MESH,
            ).start()

        each_peer(16, peer_rows, send_sums)
        pltpu.make_async_copy(sums.at[holder, b], out_ref.at[holder * 4 + b], recv5).start()
        return carry

    for h in range(2):
        half = a_mat.at[pl.ds(2 * h, 2)]
        pltpu.make_async_copy(half, half, recv3.at[h]).wait()
        lax.fori_loop(2 * h, 2 * h + 2, cross, 0)

    pltpu.make_async_copy(out_ref, out_ref, recv5).wait()
    pltpu.make_async_copy(got.at[pl.ds(0, 48)], got.at[pl.ds(0, 48)], send1).wait()
    pltpu.make_async_copy(white.at[pl.ds(0, 508)], white.at[pl.ds(0, 508)], send3).wait()
    pltpu.make_async_copy(sums.at[pl.ds(0, 31)], sums.at[pl.ds(0, 31)], send5).wait()


def order_kernel(partner_ref, in_ref, out_ref, held, wide, in_sem, out_sem):
    chan = lax.axis_index("chan")
    parts = in_sem.shape[0]
    size = in_ref.shape[0] // parts

    def fetch(i):
        span = pl.ds(i * size, size)
        return pltpu.make_async_copy(in_ref.at[span], held.at[span], in_sem.at[i])

    for i in range(parts):
        fetch(i).start()

    def body(i, carry):
        span = pl.ds(i * size, size)
        fetch(i).wait()
        for r in range(8):
            wide[r, span] = held[span, partner_ref[r, chan]].astype(jnp.float32)
        pltpu.make_async_copy(wide.at[:, span], out_ref.at[0, :, span], out_sem).start()
        return carry

    lax.fori_loop(0, parts, body, 0)
    pltpu.make_async_copy(wide, out_ref.at[0], out_sem).wait()


def per_device(samples, partner):
    table = jnp.asarray(tables())
    sums = pl.pallas_call(
        main_kernel,
        out_shape=jax.ShapeDtypeStruct((128, 8, 16, 128), jnp.bfloat16),
        in_specs=[pl.BlockSpec(memory_space=pl.ANY)] * 2,
        out_specs=pl.BlockSpec(memory_space=pl.ANY),
        scratch_shapes=[
            pltpu.VMEM((2 * BINS, LENGTH), jnp.bfloat16),
            pltpu.VMEM((SEGS, 16, LENGTH), jnp.bfloat16),
            pltpu.VMEM((ROWS, 128), jnp.float32),
            pltpu.VMEM((ROWS, LENGTH), jnp.bfloat16),
            pltpu.VMEM((2 * BINS, ROWS), jnp.float32),
            pltpu.VMEM((BINS, ROWS), jnp.bfloat16),
            pltpu.VMEM((BINS, ROWS), jnp.bfloat16),
            pltpu.VMEM((128 * 16, 128), jnp.float32),
            pltpu.VMEM((BINS, 16, 128), jnp.bfloat16),
            pltpu.VMEM((4, CHANS, 512), jnp.bfloat16),
            pltpu.VMEM((256, 512), jnp.bfloat16),
            pltpu.VMEM((32, 4, 8, 16, 128), jnp.bfloat16),
        ] + [
            pltpu.SemaphoreType.DMA, pltpu.SemaphoreType.DMA, pltpu.SemaphoreType.DMA((4,))
        ] + [
            pltpu.SemaphoreType.DMA, pltpu.SemaphoreType.DMA((2,)),
            pltpu.SemaphoreType.DMA, pltpu.SemaphoreType.DMA, pltpu.SemaphoreType.REGULAR((3,))],
        compiler_params=pltpu.CompilerParams(
            collective_id=0, has_side_effects=True, vmem_limit_bytes=60 * 2**20),
        name="spectra",
    )(samples, table)
    return pl.pallas_call(
        order_kernel,
        out_shape=jax.ShapeDtypeStruct((1, 8, 128, 16, 128), jnp.float32),
        in_specs=[
            pl.BlockSpec(memory_space=pltpu.SMEM), pl.BlockSpec(memory_space=pl.ANY)],
        out_specs=pl.BlockSpec(memory_space=pl.ANY),
        scratch_shapes=[
            pltpu.VMEM((128, 8, 16, 128), jnp.bfloat16),
            pltpu.VMEM((8, 128, 16, 128), jnp.float32),
            pltpu.SemaphoreType.DMA((16,)),
            pltpu.SemaphoreType.DMA,
        ],
        compiler_params=pltpu.CompilerParams(vmem_limit_bytes=60 * 2**20),
        name="order",
    )(partner, sums)


def solution(mesh):
    in_specs = (P("win", "chan", "freq"), P())
    out_specs = P("chan", None, "freq", "win", None)
    return jax.shard_map(
        per_device, mesh=mesh, in_specs=in_specs, out_specs=out_specs, check_vma=False
    )
```

```python
import math

import jax
import jax.numpy as jnp
import ml_dtypes
import numpy as np
from jax import lax
from jax.experimental import pallas as pl
from jax.experimental.pallas import tpu as pltpu
from jax.sharding import PartitionSpec as P

MESH = pl.DeviceIdType.MESH
NT = (((1,), (1,)), ((), ()))

LENGTH = 1024
BINS = 512
MARGIN = 64
SEGS = 64
SEGMENTS = 256
BLOCK = 64
CHANS = 512
ROWS = 1024


def tables():
    n = np.arange(LENGTH)[None, :]
    f = np.arange(BINS)[:, None]
    angle = (n * f % LENGTH) * (2.0 * math.pi / LENGTH)
    both = np.concatenate([np.cos(angle), -np.sin(angle)], axis=0) / math.sqrt(LENGTH)
    return both.astype(np.float32).astype(ml_dtypes.bfloat16)


def position():
    chan, win, freq = (lax.axis_index(name) for name in ("chan", "win", "freq"))
    return chan // 4, chan % 4, win, freq // 2, freq % 2


def spread(freq):
    y_hi, x, z, _, _ = position()
    halves = y_hi, 1 - y_hi
    xs = [(x + i) % 4 for i in range(4)]
    zs = [(z + i) % 4 for i in range(4)]
    return [
        (halves[s] * 4 + xs[(i + 2 * s) % 4], zs[(j + 2 * s) % 4], freq)
        for j in range(4) for i in range(4) for s in range(2)
    ]


def main_kernel(
    x_ref, table_ref, out_ref,
    table, got, wide, rows, spec, high, low, mixed, white, a_mat, b_mat, sums,
    table_sem, send1, recv1, send3, recv3, send5, recv5, in_sem,
):
    chan, win, freq = (lax.axis_index(name) for name in ("chan", "win", "freq"))
    holder = chan * 4 + win
    piece = x_ref.shape[2]
    take_table = pltpu.make_async_copy(table_ref, table, table_sem)
    take_table.start()

    barrier = pltpu.get_barrier_semaphore()
    y_hi, x, z, y_lo, core = position()
    along_x = [(y_hi * 4 + (x + i) % 4, win, freq) for i in (1, 2, 3)]
    along_z = [(chan, (z + i) % 4, freq) for i in (1, 2, 3)]
    along_freq = [(chan, win, (freq + i) % 4) for i in (1, 2, 3)]

    def tell(semaphore, devices):
        for d in devices:
            pl.semaphore_signal(semaphore, inc=1, device_id=d, device_id_type=MESH)

    tell(barrier, along_freq + along_x + along_z + [((1 - y_hi) * 4 + x, win, freq)])
    pl.semaphore_wait(barrier, 10)

    def across(i):
        return (y_lo + i // 2) % 2 * 2 + (core + i % 2) % 2

    def stretch(k, size=1):
        return pl.ds(pl.multiple_of(k * piece, size * piece), size * piece)

    pltpu.make_async_copy(
        x_ref.at[:, pl.ds(pl.multiple_of(freq * 16, 16), 16), :],
        got.at[:, :, stretch(freq)], recv1.at[0],
    ).start()
    for i in (2, 1, 3):
        k = across(i)
        pltpu.make_async_remote_copy(
            src_ref=x_ref.at[:, pl.ds(pl.multiple_of(k * 16, 16), 16), :],
            dst_ref=got.at[:, :, stretch(freq)],
            send_sem=send1, recv_sem=recv1.at[i],
            device_id=(chan, win, k), device_id_type=MESH,
        ).start()

    def arrived(i):
        part = got.at[:, :, stretch(across(i))]
        pltpu.make_async_copy(part, part, recv1.at[i]).wait()

    def reorder(k):
        def body(c, carry):
            at = pl.ds(pl.multiple_of(k * piece + c * 128, 128), 128)
            wide[...] = got[:, :, at].astype(jnp.float32).reshape(ROWS, 128)
            for ch in range(16):
                rows[ch * 64:(ch + 1) * 64, at] = (
                    wide[pl.ds(ch, 64, stride=16), :].astype(jnp.bfloat16))
            return carry

        lax.fori_loop(0, piece // 128, body, 0)

    def transform(k, size, first):
        span = stretch(k, size)

        def body(t, carry):
            at = pl.ds(pl.multiple_of(t * 256, 256), 256)
            term = lax.dot_general(
                table[:, span], rows[at, span], NT, preferred_element_type=jnp.float32)
            spec[:, at] = term if first else spec[:, at] + term
            return carry

        lax.fori_loop(0, ROWS // 256, body, 0)

    tell(in_sem.at[0], along_z)
    take_table.wait()
    for i in (0, 1):
        arrived(i)
        reorder(across(i))
    pl.semaphore_wait(in_sem.at[0], 3)
    tell(in_sem.at[1], along_x)
    transform(y_lo * 2, 2, True)
    pl.semaphore_wait(in_sem.at[1], 3)
    tell(in_sem.at[2], along_freq)
    arrived(2)
    reorder(across(2))
    transform(across(2), 1, False)
    arrived(3)
    reorder(across(3))

    def finish(half):
        span = stretch(across(3))
        re_at = pl.ds(pl.multiple_of(half * 256, 256), 256)
        im_at = pl.ds(pl.multiple_of(BINS + half * 256, 256), 256)

        def body(t, carry):
            at = pl.ds(pl.multiple_of(t * 256, 256), 256)

            def total(part):
                return spec[part, at] + lax.dot_general(
                    table[part, span], rows[at, span], NT, preferred_element_type=jnp.float32)

            re, im = total(re_at), total(im_at)
            spec[re_at, at] = re
            spec[im_at, at] = im
            power = re * re + im * im
            top = power.astype(jnp.bfloat16)
            high[re_at, at] = top
            low[re_at, at] = (power - top.astype(jnp.float32)).astype(jnp.bfloat16)
            return carry

        lax.fori_loop(0, ROWS // 256, body, 0)

    place_ch = pl.ds(pl.multiple_of(chan * 64 + freq * 16, 16), 16)
    place_k = pl.ds(pl.multiple_of(win * 128, 128), 128)

    def white_of(d, h):
        return white.at[pl.ds(d[2] * 128 + (d[0] * 4 + d[1]) * 4 + 2 * h, 2)]

    def send_white(h, d):
        pltpu.make_async_remote_copy(
            src_ref=white_of(d, h),
            dst_ref=a_mat.at[pl.ds(2 * h, 2), place_ch, place_k],
            send_sem=send3, recv_sem=recv3.at[h], device_id=d, device_id_type=MESH,
        ).start()

    def turn(i):
        return y_lo * 3 + (1 - 2 * y_lo) * i

    def send_share(t, h):
        own, *others = spread(t)
        pl.when(t != freq)(lambda: send_white(h, own))
        for d in others:
            send_white(h, d)

    left = lax.broadcasted_iota(jnp.int32, (128, 128), 1) < 64

    def whiten(i, carry):
        t = turn(i)
        first = t * 128
        start = jnp.clip(first - 64, 0, BINS - 256)
        window = pl.ds(pl.multiple_of(start, 64), 256)
        apart = (lax.broadcasted_iota(jnp.int32, (128, 256), 1) + start) - (
            lax.broadcasted_iota(jnp.int32, (128, 256), 0) + first)
        band = jnp.where((apart >= -MARGIN) & (apart <= MARGIN), 1.0, 0.0).astype(jnp.bfloat16)
        smooth = (
            jnp.dot(band, high[window, :], preferred_element_type=jnp.float32)
            + jnp.dot(band, low[window, :], preferred_element_type=jnp.float32)
        ) / (2 * MARGIN + 1)
        scale = lax.rsqrt(smooth + 1e-06)
        re = spec[pl.ds(pl.multiple_of(first, 128), 128), :] * scale
        im = spec[pl.ds(pl.multiple_of(BINS + first, 128), 128), :] * scale
        for c in range(8):
            a, b = re[:, c * 128:(c + 1) * 128], im[:, c * 128:(c + 1) * 128]
            mixed[pl.ds(2 * c, 128, stride=16), :] = jnp.where(left, a, pltpu.roll(b, 64, 1))
            mixed[pl.ds(2 * c + 1, 128, stride=16), :] = jnp.where(left, pltpu.roll(a, 64, 1), b)
        white[pl.ds(pl.multiple_of(first, 128), 128)] = (
            mixed[...].reshape(128, 16, 128).astype(jnp.bfloat16))
        send_share(t, 0)
        return carry

    finish(y_lo)
    pl.semaphore_wait(in_sem.at[2], 3)
    whiten(0, 0)
    finish(1 - y_lo)
    lax.fori_loop(1, BINS // 128, whiten, 0)
    for h in range(2):
        pltpu.make_async_copy(
            white_of((chan, win, freq), h), a_mat.at[pl.ds(2 * h, 2), place_ch, place_k],
            recv3.at[h],
        ).start()

    def send_rest(i, carry):
        send_share(turn(i), 1)
        return carry

    lax.fori_loop(0, 4, send_rest, 0)

    sign = jnp.where(lax.broadcasted_iota(jnp.int32, (64, 128), 1) < 64, 1.0, -1.0)

    def cross(b, carry):
        def multiply(m, c):
            for h in range(2):
                block = a_mat[b, pl.ds(pl.multiple_of(m * 128 + h * 64, 64), 64), :]
                b_mat[h * 128:h * 128 + 64, :] = block
                for w in range(4):
                    part = block[:, w * 128:(w + 1) * 128].astype(jnp.float32)
                    b_mat[h * 128 + 64:h * 128 + 128, w * 128:(w + 1) * 128] = (
                        pltpu.roll(part, 64, 1) * sign).astype(jnp.bfloat16)
            tile = lax.dot_general(
                a_mat[b], b_mat[...], NT, preferred_element_type=jnp.float32)
            tile = (tile * (1.0 / SEGMENTS)).astype(jnp.bfloat16)
            for h in range(2):
                sums[:, b, m * 2 + h] = tile[:, h * 128:(h + 1) * 128].reshape(32, 16, 128)
            return c

        lax.fori_loop(0, 4, multiply, 0)

        def send_sums(d):
            pltpu.make_async_remote_copy(
                src_ref=sums.at[d[0] * 4 + d[1], b],
                dst_ref=out_ref.at[holder * 4 + b],
                send_sem=send5, recv_sem=recv5, device_id=d, device_id_type=MESH,
            ).start()

        for d in spread(freq)[1:]:
            send_sums(d)
        pltpu.make_async_copy(sums.at[holder, b], out_ref.at[holder * 4 + b], recv5).start()
        return carry

    for h in range(2):
        half = a_mat.at[pl.ds(2 * h, 2)]
        pltpu.make_async_copy(half, half, recv3.at[h]).wait()
        lax.fori_loop(2 * h, 2 * h + 2, cross, 0)

    pltpu.make_async_copy(out_ref, out_ref, recv5).wait()
    pltpu.make_async_copy(got.at[pl.ds(0, 48)], got.at[pl.ds(0, 48)], send1).wait()
    pltpu.make_async_copy(white.at[pl.ds(0, 508)], white.at[pl.ds(0, 508)], send3).wait()
    pltpu.make_async_copy(sums.at[pl.ds(0, 31)], sums.at[pl.ds(0, 31)], send5).wait()


def order_kernel(partner_ref, in_ref, out_ref, wide, out_sem):
    chan = lax.axis_index("chan")
    parts = 8
    size = in_ref.shape[0] // parts

    def body(i, carry):
        span = pl.ds(i * size, size)
        for r in range(8):
            wide[r, span] = in_ref[span, partner_ref[r, chan]].astype(jnp.float32)
        pltpu.make_async_copy(wide.at[:, span], out_ref.at[0, :, span], out_sem).start()
        return carry

    lax.fori_loop(0, parts, body, 0)
    pltpu.make_async_copy(wide, out_ref.at[0], out_sem).wait()


def per_device(samples, partner):
    table = jnp.asarray(tables())
    sums = pl.pallas_call(
        main_kernel,
        out_shape=pltpu.VMEM((128, 8, 16, 128), jnp.bfloat16),
        in_specs=[pl.BlockSpec(memory_space=pl.ANY)] * 2,
        out_specs=pl.BlockSpec(memory_space=pltpu.VMEM),
        scratch_shapes=[
            pltpu.VMEM((2 * BINS, LENGTH), jnp.bfloat16),
            pltpu.VMEM((SEGS, 16, LENGTH), jnp.bfloat16),
            pltpu.VMEM((ROWS, 128), jnp.float32),
            pltpu.VMEM((ROWS, LENGTH), jnp.bfloat16),
            pltpu.VMEM((2 * BINS, ROWS), jnp.float32),
            pltpu.VMEM((BINS, ROWS), jnp.bfloat16),
            pltpu.VMEM((BINS, ROWS), jnp.bfloat16),
            pltpu.VMEM((128 * 16, 128), jnp.float32),
            pltpu.VMEM((BINS, 16, 128), jnp.bfloat16),
            pltpu.VMEM((4, CHANS, 512), jnp.bfloat16),
            pltpu.VMEM((256, 512), jnp.bfloat16),
            pltpu.VMEM((32, 4, 8, 16, 128), jnp.bfloat16),
        ] + [
            pltpu.SemaphoreType.DMA, pltpu.SemaphoreType.DMA, pltpu.SemaphoreType.DMA((4,))
        ] + [
            pltpu.SemaphoreType.DMA, pltpu.SemaphoreType.DMA((2,)),
            pltpu.SemaphoreType.DMA, pltpu.SemaphoreType.DMA, pltpu.SemaphoreType.REGULAR((3,))],
        compiler_params=pltpu.CompilerParams(
            collective_id=0, has_side_effects=True, vmem_limit_bytes=50 * 2**20),
        name="spectra",
    )(samples, table)
    return pl.pallas_call(
        order_kernel,
        out_shape=jax.ShapeDtypeStruct((1, 8, 128, 16, 128), jnp.float32),
        in_specs=[
            pl.BlockSpec(memory_space=pltpu.SMEM), pl.BlockSpec(memory_space=pltpu.VMEM)],
        out_specs=pl.BlockSpec(memory_space=pl.ANY),
        scratch_shapes=[
            pltpu.VMEM((8, 128, 16, 128), jnp.float32),
            pltpu.SemaphoreType.DMA,
        ],
        compiler_params=pltpu.CompilerParams(vmem_limit_bytes=20 * 2**20),
        name="order",
    )(partner, sums)


def solution(mesh):
    in_specs = (P("win", "chan", "freq"), P())
    out_specs = P("chan", None, "freq", "win", None)
    return jax.shard_map(
        per_device, mesh=mesh, in_specs=in_specs, out_specs=out_specs, check_vma=False
    )
```

```python
import math

import jax
import jax.numpy as jnp
import ml_dtypes
import numpy as np
from jax import lax
from jax.experimental import pallas as pl
from jax.experimental.pallas import tpu as pltpu
from jax.sharding import PartitionSpec as P

MESH = pl.DeviceIdType.MESH
NT = (((1,), (1,)), ((), ()))

LENGTH = 1024
BINS = 512
MARGIN = 64
SEGS = 64
SEGMENTS = 256
BLOCK = 64
CHANS = 512
ROWS = 1024


def tables():
    n = np.arange(LENGTH)[None, :]
    f = np.arange(BINS)[:, None]
    angle = (n * f % LENGTH) * (2.0 * math.pi / LENGTH)
    both = np.concatenate([np.cos(angle), -np.sin(angle)], axis=0) / math.sqrt(LENGTH)
    return both.astype(np.float32).astype(ml_dtypes.bfloat16)


def position():
    chan, win, freq = (lax.axis_index(name) for name in ("chan", "win", "freq"))
    return chan // 4, chan % 4, win, freq // 2, freq % 2


def spread(freq):
    y_hi, x, z, _, _ = position()
    halves = y_hi, 1 - y_hi
    xs = [(x + i) % 4 for i in range(4)]
    zs = [(z + i) % 4 for i in range(4)]
    return [
        (halves[s] * 4 + xs[(i + 2 * s) % 4], zs[(j + 2 * s) % 4], freq)
        for j in range(4) for i in range(4) for s in range(2)
    ]


def main_kernel(
    x_ref, table_ref, out_ref,
    table, got, wide, rows, spec, high, low, mixed, white, a_mat, b_mat, sums,
    table_sem, send1, recv1, send3, recv3, send5, recv5, in_sem,
):
    chan, win, freq = (lax.axis_index(name) for name in ("chan", "win", "freq"))
    holder = chan * 4 + win
    piece = x_ref.shape[2]
    take_table = pltpu.make_async_copy(table_ref, table, table_sem)
    take_table.start()

    barrier = pltpu.get_barrier_semaphore()
    y_hi, x, z, y_lo, core = position()
    along_x = [(y_hi * 4 + (x + i) % 4, win, freq) for i in (1, 2, 3)]
    along_z = [(chan, (z + i) % 4, freq) for i in (1, 2, 3)]
    along_freq = [(chan, win, (freq + i) % 4) for i in (1, 2, 3)]

    def tell(semaphore, devices):
        for d in devices:
            pl.semaphore_signal(semaphore, inc=1, device_id=d, device_id_type=MESH)

    tell(barrier, along_freq + along_x + along_z + [((1 - y_hi) * 4 + x, win, freq)])
    pl.semaphore_wait(barrier, 10)

    def across(i):
        return (y_lo + i // 2) % 2 * 2 + (core + i % 2) % 2

    def stretch(k, size=1):
        return pl.ds(pl.multiple_of(k * piece, size * piece), size * piece)

    for i in (2, 3, 1):
        k = across(i)
        pltpu.make_async_remote_copy(
            src_ref=x_ref.at[:, pl.ds(pl.multiple_of(k * 16, 16), 16), :],
            dst_ref=got.at[:, :, stretch(freq)],
            send_sem=send1, recv_sem=recv1.at[i],
            device_id=(chan, win, k), device_id_type=MESH,
        ).start()

    pltpu.make_async_copy(
        x_ref.at[:, pl.ds(pl.multiple_of(freq * 16, 16), 16), :],
        got.at[:, :, stretch(freq)], recv1.at[0],
    ).start()

    def arrived(i):
        part = got.at[:, :, stretch(across(i))]
        pltpu.make_async_copy(part, part, recv1.at[i]).wait()

    def reorder(k):
        def body(c, carry):
            at = pl.ds(pl.multiple_of(k * piece + c * 128, 128), 128)
            wide[...] = got[:, :, at].astype(jnp.float32).reshape(ROWS, 128)
            for ch in range(16):
                rows[ch * 64:(ch + 1) * 64, at] = (
                    wide[pl.ds(ch, 64, stride=16), :].astype(jnp.bfloat16))
            return carry

        lax.fori_loop(0, piece // 128, body, 0)

    def transform(k, size, first):
        span = stretch(k, size)

        def body(t, carry):
            at = pl.ds(pl.multiple_of(t * 256, 256), 256)
            term = lax.dot_general(
                table[:, span], rows[at, span], NT, preferred_element_type=jnp.float32)
            spec[:, at] = term if first else spec[:, at] + term
            return carry

        lax.fori_loop(0, ROWS // 256, body, 0)

    tell(in_sem.at[0], along_z)
    take_table.wait()
    for i in (0, 1):
        arrived(i)
        reorder(across(i))
    pl.semaphore_wait(in_sem.at[0], 3)
    tell(in_sem.at[1], along_x)
    transform(y_lo * 2, 2, True)
    pl.semaphore_wait(in_sem.at[1], 3)
    tell(in_sem.at[2], along_freq)
    arrived(2)
    reorder(across(2))
    transform(across(2), 1, False)
    arrived(3)
    reorder(across(3))

    def finish(half):
        span = stretch(across(3))
        re_at = pl.ds(pl.multiple_of(half * 256, 256), 256)
        im_at = pl.ds(pl.multiple_of(BINS + half * 256, 256), 256)

        def body(t, carry):
            at = pl.ds(pl.multiple_of(t * 256, 256), 256)

            def total(part):
                return spec[part, at] + lax.dot_general(
                    table[part, span], rows[at, span], NT, preferred_element_type=jnp.float32)

            re, im = total(re_at), total(im_at)
            spec[re_at, at] = re
            spec[im_at, at] = im
            power = re * re + im * im
            top = power.astype(jnp.bfloat16)
            high[re_at, at] = top
            low[re_at, at] = (power - top.astype(jnp.float32)).astype(jnp.bfloat16)
            return carry

        lax.fori_loop(0, ROWS // 256, body, 0)

    place_ch = pl.ds(pl.multiple_of(chan * 64 + freq * 16, 16), 16)
    place_k = pl.ds(pl.multiple_of(win * 128, 128), 128)

    def white_of(d, h):
        return white.at[pl.ds(d[2] * 128 + (d[0] * 4 + d[1]) * 4 + 2 * h, 2)]

    def send_white(h, d):
        pltpu.make_async_remote_copy(
            src_ref=white_of(d, h),
            dst_ref=a_mat.at[pl.ds(2 * h, 2), place_ch, place_k],
            send_sem=send3, recv_sem=recv3.at[h], device_id=d, device_id_type=MESH,
        ).start()

    def turn(i):
        return y_lo * 3 + (1 - 2 * y_lo) * i

    def send_share(t, h):
        own, *others = spread(t)
        pl.when(t != freq)(lambda: send_white(h, own))
        for d in others:
            send_white(h, d)

    left = lax.broadcasted_iota(jnp.int32, (128, 128), 1) < 64

    def whiten(i, carry):
        t = turn(i)
        first = t * 128
        start = jnp.clip(first - 64, 0, BINS - 256)
        window = pl.ds(pl.multiple_of(start, 64), 256)
        apart = (lax.broadcasted_iota(jnp.int32, (128, 256), 1) + start) - (
            lax.broadcasted_iota(jnp.int32, (128, 256), 0) + first)
        band = jnp.where((apart >= -MARGIN) & (apart <= MARGIN), 1.0, 0.0).astype(jnp.bfloat16)
        smooth = (
            jnp.dot(band, high[window, :], preferred_element_type=jnp.float32)
            + jnp.dot(band, low[window, :], preferred_element_type=jnp.float32)
        ) / (2 * MARGIN + 1)
        scale = lax.rsqrt(smooth + 1e-06)
        re = spec[pl.ds(pl.multiple_of(first, 128), 128), :] * scale
        im = spec[pl.ds(pl.multiple_of(BINS + first, 128), 128), :] * scale
        for c in range(8):
            a, b = re[:, c * 128:(c + 1) * 128], im[:, c * 128:(c + 1) * 128]
            mixed[pl.ds(2 * c, 128, stride=16), :] = jnp.where(left, a, pltpu.roll(b, 64, 1))
            mixed[pl.ds(2 * c + 1, 128, stride=16), :] = jnp.where(left, pltpu.roll(a, 64, 1), b)
        white[pl.ds(pl.multiple_of(first, 128), 128)] = (
            mixed[...].reshape(128, 16, 128).astype(jnp.bfloat16))
        send_share(t, 0)
        send_share(t, 1)
        return carry

    finish(y_lo)
    pl.semaphore_wait(in_sem.at[2], 3)
    whiten(0, 0)
    finish(1 - y_lo)
    lax.fori_loop(1, BINS // 128, whiten, 0)
    for h in range(2):
        pltpu.make_async_copy(
            white_of((chan, win, freq), h), a_mat.at[pl.ds(2 * h, 2), place_ch, place_k],
            recv3.at[h],
        ).start()

    sign = jnp.where(lax.broadcasted_iota(jnp.int32, (64, 128), 1) < 64, 1.0, -1.0)

    def cross(b, carry):
        def multiply(m, c):
            for h in range(2):
                block = a_mat[b, pl.ds(pl.multiple_of(m * 128 + h * 64, 64), 64), :]
                b_mat[h * 128:h * 128 + 64, :] = block
                for w in range(4):
                    part = block[:, w * 128:(w + 1) * 128].astype(jnp.float32)
                    b_mat[h * 128 + 64:h * 128 + 128, w * 128:(w + 1) * 128] = (
                        pltpu.roll(part, 64, 1) * sign).astype(jnp.bfloat16)
            tile = lax.dot_general(
                a_mat[b], b_mat[...], NT, preferred_element_type=jnp.float32)
            tile = (tile * (1.0 / SEGMENTS)).astype(jnp.bfloat16)
            for h in range(2):
                sums[:, b, m * 2 + h] = tile[:, h * 128:(h + 1) * 128].reshape(32, 16, 128)
            return c

        lax.fori_loop(0, 4, multiply, 0)

        def send_sums(d):
            pltpu.make_async_remote_copy(
                src_ref=sums.at[d[0] * 4 + d[1], b],
                dst_ref=out_ref.at[holder * 4 + b],
                send_sem=send5, recv_sem=recv5, device_id=d, device_id_type=MESH,
            ).start()

        for d in spread(freq)[1:]:
            send_sums(d)
        pltpu.make_async_copy(sums.at[holder, b], out_ref.at[holder * 4 + b], recv5).start()
        return carry

    for h in range(2):
        half = a_mat.at[pl.ds(2 * h, 2)]
        pltpu.make_async_copy(half, half, recv3.at[h]).wait()
        lax.fori_loop(2 * h, 2 * h + 2, cross, 0)

    pltpu.make_async_copy(out_ref, out_ref, recv5).wait()
    pltpu.make_async_copy(got.at[pl.ds(0, 48)], got.at[pl.ds(0, 48)], send1).wait()
    pltpu.make_async_copy(white.at[pl.ds(0, 508)], white.at[pl.ds(0, 508)], send3).wait()
    pltpu.make_async_copy(sums.at[pl.ds(0, 31)], sums.at[pl.ds(0, 31)], send5).wait()


def order_kernel(partner_ref, in_ref, out_ref, wide, out_sem):
    chan = lax.axis_index("chan")
    parts = 8
    size = in_ref.shape[0] // parts

    def body(i, carry):
        span = pl.ds(i * size, size)
        for r in range(8):
            wide[r, span] = in_ref[span, partner_ref[r, chan]].astype(jnp.float32)
        pltpu.make_async_copy(wide.at[:, span], out_ref.at[0, :, span], out_sem).start()
        return carry

    lax.fori_loop(0, parts, body, 0)
    pltpu.make_async_copy(wide, out_ref.at[0], out_sem).wait()


def per_device(samples, partner):
    table = jnp.asarray(tables())
    sums = pl.pallas_call(
        main_kernel,
        out_shape=pltpu.VMEM((128, 8, 16, 128), jnp.bfloat16),
        in_specs=[pl.BlockSpec(memory_space=pl.ANY)] * 2,
        out_specs=pl.BlockSpec(memory_space=pltpu.VMEM),
        scratch_shapes=[
            pltpu.VMEM((2 * BINS, LENGTH), jnp.bfloat16),
            pltpu.VMEM((SEGS, 16, LENGTH), jnp.bfloat16),
            pltpu.VMEM((ROWS, 128), jnp.float32),
            pltpu.VMEM((ROWS, LENGTH), jnp.bfloat16),
            pltpu.VMEM((2 * BINS, ROWS), jnp.float32),
            pltpu.VMEM((BINS, ROWS), jnp.bfloat16),
            pltpu.VMEM((BINS, ROWS), jnp.bfloat16),
            pltpu.VMEM((128 * 16, 128), jnp.float32),
            pltpu.VMEM((BINS, 16, 128), jnp.bfloat16),
            pltpu.VMEM((4, CHANS, 512), jnp.bfloat16),
            pltpu.VMEM((256, 512), jnp.bfloat16),
            pltpu.VMEM((32, 4, 8, 16, 128), jnp.bfloat16),
        ] + [
            pltpu.SemaphoreType.DMA, pltpu.SemaphoreType.DMA, pltpu.SemaphoreType.DMA((4,))
        ] + [
            pltpu.SemaphoreType.DMA, pltpu.SemaphoreType.DMA((2,)),
            pltpu.SemaphoreType.DMA, pltpu.SemaphoreType.DMA, pltpu.SemaphoreType.REGULAR((3,))],
        compiler_params=pltpu.CompilerParams(
            collective_id=0, has_side_effects=True, vmem_limit_bytes=50 * 2**20),
        name="spectra",
    )(samples, table)
    return pl.pallas_call(
        order_kernel,
        out_shape=jax.ShapeDtypeStruct((1, 8, 128, 16, 128), jnp.float32),
        in_specs=[
            pl.BlockSpec(memory_space=pltpu.SMEM), pl.BlockSpec(memory_space=pltpu.VMEM)],
        out_specs=pl.BlockSpec(memory_space=pl.ANY),
        scratch_shapes=[
            pltpu.VMEM((8, 128, 16, 128), jnp.float32),
            pltpu.SemaphoreType.DMA,
        ],
        compiler_params=pltpu.CompilerParams(vmem_limit_bytes=20 * 2**20),
        name="order",
    )(partner, sums)


def solution(mesh):
    in_specs = (P("win", "chan", "freq"), P())
    out_specs = P("chan", None, "freq", "win", None)
    return jax.shard_map(
        per_device, mesh=mesh, in_specs=in_specs, out_specs=out_specs, check_vma=False
    )
```

```python
import math

import jax
import jax.numpy as jnp
import ml_dtypes
import numpy as np
from jax import lax
from jax.experimental import pallas as pl
from jax.experimental.pallas import tpu as pltpu
from jax.sharding import PartitionSpec as P

MESH = pl.DeviceIdType.MESH
NT = (((1,), (1,)), ((), ()))

LENGTH = 1024
BINS = 512
MARGIN = 64
SEGS = 64
SEGMENTS = 256
BLOCK = 64
CHANS = 512
ROWS = 1024


def tables():
    n = np.arange(LENGTH)[None, :]
    f = np.arange(BINS)[:, None]
    angle = (n * f % LENGTH) * (2.0 * math.pi / LENGTH)
    both = np.concatenate([np.cos(angle), -np.sin(angle)], axis=0) / math.sqrt(LENGTH)
    return both.astype(np.float32).astype(ml_dtypes.bfloat16)


def position():
    chan, win, freq = (lax.axis_index(name) for name in ("chan", "win", "freq"))
    return chan // 4, chan % 4, win, freq // 2, freq % 2


def spread(freq):
    y_hi, x, z, _, _ = position()
    halves = y_hi, 1 - y_hi
    xs = [(x + i) % 4 for i in range(4)]
    zs = [(z + i) % 4 for i in range(4)]
    return [
        (halves[s] * 4 + xs[(i + 2 * s) % 4], zs[(j + 2 * s) % 4], freq)
        for j in range(4) for i in range(4) for s in range(2)
    ]


def main_kernel(
    x_ref, table_ref, out_ref,
    table, got, wide, rows, spec, high, low, mixed, white, a_mat, b_mat, sums,
    table_sem, send1, recv1, send3, recv3, send5, recv5, in_sem,
):
    chan, win, freq = (lax.axis_index(name) for name in ("chan", "win", "freq"))
    holder = chan * 4 + win
    piece = x_ref.shape[2]
    take_table = pltpu.make_async_copy(table_ref, table, table_sem)
    take_table.start()

    barrier = pltpu.get_barrier_semaphore()
    y_hi, x, z, y_lo, core = position()
    along_x = [(y_hi * 4 + (x + i) % 4, win, freq) for i in (1, 2, 3)]
    along_z = [(chan, (z + i) % 4, freq) for i in (1, 2, 3)]
    along_freq = [(chan, win, (freq + i) % 4) for i in (1, 2, 3)]

    def tell(semaphore, devices):
        for d in devices:
            pl.semaphore_signal(semaphore, inc=1, device_id=d, device_id_type=MESH)

    tell(barrier, along_freq + along_x + along_z + [((1 - y_hi) * 4 + x, win, freq)])
    pl.semaphore_wait(barrier, 10)

    def across(i):
        return (y_lo + i // 2) % 2 * 2 + (core + i % 2) % 2

    def stretch(k, size=1):
        return pl.ds(pl.multiple_of(k * piece, size * piece), size * piece)

    for i in (2, 3, 1):
        k = across(i)
        pltpu.make_async_remote_copy(
            src_ref=x_ref.at[:, pl.ds(pl.multiple_of(k * 16, 16), 16), :],
            dst_ref=got.at[:, :, stretch(freq)],
            send_sem=send1, recv_sem=recv1.at[i],
            device_id=(chan, win, k), device_id_type=MESH,
        ).start()

    pltpu.make_async_copy(
        x_ref.at[:, pl.ds(pl.multiple_of(freq * 16, 16), 16), :],
        got.at[:, :, stretch(freq)], recv1.at[0],
    ).start()

    def arrived(i):
        part = got.at[:, :, stretch(across(i))]
        pltpu.make_async_copy(part, part, recv1.at[i]).wait()

    def reorder(k):
        def body(c, carry):
            at = pl.ds(pl.multiple_of(k * piece + c * 128, 128), 128)
            wide[:ROWS, :] = got[:, :, at].astype(jnp.float32).reshape(ROWS, 128)
            for ch in range(16):
                rows[ch * 64:(ch + 1) * 64, at] = (
                    wide[pl.ds(ch, 64, stride=16), :].astype(jnp.bfloat16))
            return carry

        lax.fori_loop(0, piece // 128, body, 0)

    def transform(k, size, first):
        span = stretch(k, size)

        def body(t, carry):
            at = pl.ds(pl.multiple_of(t * 256, 256), 256)
            term = lax.dot_general(
                table[:, span], rows[at, span], NT, preferred_element_type=jnp.float32)
            spec[:, at] = term if first else spec[:, at] + term
            return carry

        lax.fori_loop(0, ROWS // 256, body, 0)

    tell(in_sem.at[0], along_z)
    take_table.wait()
    for i in (0, 1):
        arrived(i)
        reorder(across(i))
    pl.semaphore_wait(in_sem.at[0], 3)
    tell(in_sem.at[1], along_x)
    transform(y_lo * 2, 2, True)
    pl.semaphore_wait(in_sem.at[1], 3)
    tell(in_sem.at[2], along_freq)
    arrived(2)
    reorder(across(2))
    transform(across(2), 1, False)
    arrived(3)
    reorder(across(3))

    def finish(half):
        span = stretch(across(3))
        re_at = pl.ds(pl.multiple_of(half * 256, 256), 256)
        im_at = pl.ds(pl.multiple_of(BINS + half * 256, 256), 256)

        def body(t, carry):
            at = pl.ds(pl.multiple_of(t * 256, 256), 256)

            def total(part):
                return spec[part, at] + lax.dot_general(
                    table[part, span], rows[at, span], NT, preferred_element_type=jnp.float32)

            re, im = total(re_at), total(im_at)
            spec[re_at, at] = re
            spec[im_at, at] = im
            power = re * re + im * im
            top = power.astype(jnp.bfloat16)
            high[re_at, at] = top
            low[re_at, at] = (power - top.astype(jnp.float32)).astype(jnp.bfloat16)
            return carry

        lax.fori_loop(0, ROWS // 256, body, 0)

    place_ch = pl.ds(pl.multiple_of(chan * 64 + freq * 16, 16), 16)
    place_k = pl.ds(pl.multiple_of(win * 128, 128), 128)

    def white_of(d, h):
        return white.at[pl.ds(d[2] * 128 + (d[0] * 4 + d[1]) * 4 + 2 * h, 2)]

    def send_white(h, d):
        pltpu.make_async_remote_copy(
            src_ref=white_of(d, h),
            dst_ref=a_mat.at[pl.ds(2 * h, 2), place_ch, place_k],
            send_sem=send3, recv_sem=recv3.at[h], device_id=d, device_id_type=MESH,
        ).start()

    def turn(i):
        return y_lo * 3 + (1 - 2 * y_lo) * i

    def send_share(t, h):
        own, *others = spread(t)
        pl.when(t != freq)(lambda: send_white(h, own))
        for d in others:
            send_white(h, d)

    left = lax.broadcasted_iota(jnp.int32, (128, 128), 1) < 64

    def whiten(i, carry):
        t = turn(i)
        first = t * 128
        start = jnp.clip(first - 64, 0, BINS - 256)
        window = pl.ds(pl.multiple_of(start, 64), 256)
        apart = (lax.broadcasted_iota(jnp.int32, (128, 256), 1) + start) - (
            lax.broadcasted_iota(jnp.int32, (128, 256), 0) + first)
        band = jnp.where((apart >= -MARGIN) & (apart <= MARGIN), 1.0, 0.0).astype(jnp.bfloat16)
        smooth = (
            jnp.dot(band, high[window, :], preferred_element_type=jnp.float32)
            + jnp.dot(band, low[window, :], preferred_element_type=jnp.float32)
        ) / (2 * MARGIN + 1)
        scale = lax.rsqrt(smooth + 1e-06)
        re = spec[pl.ds(pl.multiple_of(first, 128), 128), :] * scale
        im = spec[pl.ds(pl.multiple_of(BINS + first, 128), 128), :] * scale
        for c in range(8):
            a, b = re[:, c * 128:(c + 1) * 128], im[:, c * 128:(c + 1) * 128]
            mixed[pl.ds(2 * c, 128, stride=16), :] = jnp.where(left, a, pltpu.roll(b, 64, 1))
            mixed[pl.ds(2 * c + 1, 128, stride=16), :] = jnp.where(left, pltpu.roll(a, 64, 1), b)
        white[pl.ds(pl.multiple_of(first, 128), 128)] = (
            mixed[:128 * 16, :].reshape(128, 16, 128).astype(jnp.bfloat16))
        send_share(t, 0)
        send_share(t, 1)
        return carry

    finish(y_lo)
    pl.semaphore_wait(in_sem.at[2], 3)
    whiten(0, 0)
    finish(1 - y_lo)
    lax.fori_loop(1, BINS // 128, whiten, 0)
    for h in range(2):
        pltpu.make_async_copy(
            white_of((chan, win, freq), h), a_mat.at[pl.ds(2 * h, 2), place_ch, place_k],
            recv3.at[h],
        ).start()

    sign = jnp.where(lax.broadcasted_iota(jnp.int32, (64, 128), 1) < 64, 1.0, -1.0)

    def cross(b, carry):
        def multiply(m, c):
            for h in range(2):
                block = a_mat[b, pl.ds(pl.multiple_of(m * 128 + h * 64, 64), 64), :]
                b_mat[h * 128:h * 128 + 64, :] = block
                for w in range(4):
                    part = block[:, w * 128:(w + 1) * 128].astype(jnp.float32)
                    b_mat[h * 128 + 64:h * 128 + 128, w * 128:(w + 1) * 128] = (
                        pltpu.roll(part, 64, 1) * sign).astype(jnp.bfloat16)
            tile = lax.dot_general(
                a_mat[b], b_mat[...], NT, preferred_element_type=jnp.float32)
            tile = (tile * (1.0 / SEGMENTS)).astype(jnp.bfloat16)
            for h in range(2):
                sums[:, b, m * 2 + h] = tile[:, h * 128:(h + 1) * 128].reshape(32, 16, 128)
            return c

        lax.fori_loop(0, 4, multiply, 0)

        def send_sums(d):
            pltpu.make_async_remote_copy(
                src_ref=sums.at[d[0] * 4 + d[1], b],
                dst_ref=out_ref.at[holder * 4 + b],
                send_sem=send5, recv_sem=recv5, device_id=d, device_id_type=MESH,
            ).start()

        for d in spread(freq)[1:]:
            send_sums(d)
        pltpu.make_async_copy(sums.at[holder, b], out_ref.at[holder * 4 + b], recv5).start()
        return carry

    for h in range(2):
        half = a_mat.at[pl.ds(2 * h, 2)]
        pltpu.make_async_copy(half, half, recv3.at[h]).wait()
        lax.fori_loop(2 * h, 2 * h + 2, cross, 0)

    pltpu.make_async_copy(out_ref, out_ref, recv5).wait()
    pltpu.make_async_copy(got.at[pl.ds(0, 48)], got.at[pl.ds(0, 48)], send1).wait()
    pltpu.make_async_copy(white.at[pl.ds(0, 508)], white.at[pl.ds(0, 508)], send3).wait()
    pltpu.make_async_copy(sums.at[pl.ds(0, 31)], sums.at[pl.ds(0, 31)], send5).wait()


def order_kernel(partner_ref, in_ref, out_ref, wide, out_sem):
    chan = lax.axis_index("chan")
    parts = 8
    size = in_ref.shape[0] // parts

    def body(i, carry):
        span = pl.ds(i * size, size)
        for r in range(8):
            wide[r, span] = in_ref[span, partner_ref[r, chan]].astype(jnp.float32)
            pltpu.make_async_copy(wide.at[r, span], out_ref.at[0, r, span], out_sem).start()
        return carry

    lax.fori_loop(0, parts, body, 0)
    pltpu.make_async_copy(wide, out_ref.at[0], out_sem).wait()


def per_device(samples, partner):
    table = jnp.asarray(tables())
    sums = pl.pallas_call(
        main_kernel,
        out_shape=pltpu.VMEM((128, 8, 16, 128), jnp.bfloat16),
        in_specs=[pl.BlockSpec(memory_space=pl.ANY)] * 2,
        out_specs=pl.BlockSpec(memory_space=pltpu.VMEM),
        scratch_shapes=[
            pltpu.VMEM((2 * BINS, LENGTH), jnp.bfloat16),
            pltpu.VMEM((SEGS, 16, LENGTH), jnp.bfloat16),
            pltpu.VMEM((ROWS + 16, 128), jnp.float32),
            pltpu.VMEM((ROWS, LENGTH), jnp.bfloat16),
            pltpu.VMEM((2 * BINS, ROWS), jnp.float32),
            pltpu.VMEM((BINS, ROWS), jnp.bfloat16),
            pltpu.VMEM((BINS, ROWS), jnp.bfloat16),
            pltpu.VMEM((128 * 16 + 16, 128), jnp.float32),
            pltpu.VMEM((BINS, 16, 128), jnp.bfloat16),
            pltpu.VMEM((4, CHANS, 512), jnp.bfloat16),
            pltpu.VMEM((256, 512), jnp.bfloat16),
            pltpu.VMEM((32, 4, 8, 16, 128), jnp.bfloat16),
        ] + [
            pltpu.SemaphoreType.DMA, pltpu.SemaphoreType.DMA, pltpu.SemaphoreType.DMA((4,))
        ] + [
            pltpu.SemaphoreType.DMA, pltpu.SemaphoreType.DMA((2,)),
            pltpu.SemaphoreType.DMA, pltpu.SemaphoreType.DMA, pltpu.SemaphoreType.REGULAR((3,))],
        compiler_params=pltpu.CompilerParams(
            collective_id=0, has_side_effects=True, vmem_limit_bytes=50 * 2**20),
        name="spectra",
    )(samples, table)
    return pl.pallas_call(
        order_kernel,
        out_shape=jax.ShapeDtypeStruct((1, 8, 128, 16, 128), jnp.float32),
        in_specs=[
            pl.BlockSpec(memory_space=pltpu.SMEM), pl.BlockSpec(memory_space=pltpu.VMEM)],
        out_specs=pl.BlockSpec(memory_space=pl.ANY),
        scratch_shapes=[
            pltpu.VMEM((8, 128, 16, 128), jnp.float32),
            pltpu.SemaphoreType.DMA,
        ],
        compiler_params=pltpu.CompilerParams(vmem_limit_bytes=20 * 2**20),
        name="order",
    )(partner, sums)


def solution(mesh):
    in_specs = (P("win", "chan", "freq"), P())
    out_specs = P("chan", None, "freq", "win", None)
    return jax.shard_map(
        per_device, mesh=mesh, in_specs=in_specs, out_specs=out_specs, check_vma=False
    )
```

```python
import math

import jax
import jax.numpy as jnp
import ml_dtypes
import numpy as np
from jax import lax
from jax.experimental import pallas as pl
from jax.experimental.pallas import tpu as pltpu
from jax.sharding import PartitionSpec as P

MESH = pl.DeviceIdType.MESH
NT = (((1,), (1,)), ((), ()))

LENGTH = 1024
BINS = 512
MARGIN = 64
SEGS = 64
SEGMENTS = 256
BLOCK = 64
CHANS = 512
ROWS = 1024


def tables():
    n = np.arange(LENGTH)[None, :]
    f = np.arange(BINS)[:, None]
    angle = (n * f % LENGTH) * (2.0 * math.pi / LENGTH)
    both = np.concatenate([np.cos(angle), -np.sin(angle)], axis=0) / math.sqrt(LENGTH)
    return both.astype(np.float32).astype(ml_dtypes.bfloat16)


def position():
    chan, win, freq = (lax.axis_index(name) for name in ("chan", "win", "freq"))
    return chan // 4, chan % 4, win, freq // 2, freq % 2


def spread(freq):
    y_hi, x, z, _, _ = position()
    halves = y_hi, 1 - y_hi
    xs = [(x + i) % 4 for i in range(4)]
    zs = [(z + i) % 4 for i in range(4)]
    return [
        (halves[s] * 4 + xs[(i + 2 * s) % 4], zs[(j + 2 * s) % 4], freq)
        for j in range(4) for i in range(4) for s in range(2)
    ]


def main_kernel(
    x_ref, table_ref, out_ref,
    table, got, wide, rows, spec, high, low, mixed, white, a_mat, b_mat, sums,
    table_sem, send1, recv1, send3, recv3, send5, recv5, in_sem,
):
    chan, win, freq = (lax.axis_index(name) for name in ("chan", "win", "freq"))
    holder = chan * 4 + win
    piece = x_ref.shape[2]
    take_table = pltpu.make_async_copy(table_ref, table, table_sem)
    take_table.start()

    barrier = pltpu.get_barrier_semaphore()
    y_hi, x, z, y_lo, core = position()
    along_x = [(y_hi * 4 + (x + i) % 4, win, freq) for i in (1, 2, 3)]
    along_z = [(chan, (z + i) % 4, freq) for i in (1, 2, 3)]
    along_freq = [(chan, win, (freq + i) % 4) for i in (1, 2, 3)]

    def tell(semaphore, devices):
        for d in devices:
            pl.semaphore_signal(semaphore, inc=1, device_id=d, device_id_type=MESH)

    tell(barrier, along_freq + along_x + along_z + [((1 - y_hi) * 4 + x, win, freq)])
    pl.semaphore_wait(barrier, 10)

    def across(i):
        return (y_lo + i // 2) % 2 * 2 + (core + i % 2) % 2

    def stretch(k, size=1):
        return pl.ds(pl.multiple_of(k * piece, size * piece), size * piece)

    def part(k, j, parts):
        size = piece // parts
        return pl.ds(pl.multiple_of(k * piece + j * size, size), size)

    for i, j, parts in ((2, 0, 1), (3, 0, 2), (3, 1, 2), (1, 0, 1)):
        k = across(i)
        pltpu.make_async_remote_copy(
            src_ref=x_ref.at[:, pl.ds(pl.multiple_of(k * 16, 16), 16), part(0, j, parts)],
            dst_ref=got.at[:, :, part(freq, j, parts)],
            send_sem=send1, recv_sem=recv1.at[i + j],
            device_id=(chan, win, k), device_id_type=MESH,
        ).start()

    pltpu.make_async_copy(
        x_ref.at[:, pl.ds(pl.multiple_of(freq * 16, 16), 16), :],
        got.at[:, :, stretch(freq)], recv1.at[0],
    ).start()

    def arrived(i, j=0, parts=1):
        here = got.at[:, :, part(across(i), j, parts)]
        pltpu.make_async_copy(here, here, recv1.at[i + j]).wait()

    def reorder(k, j=0, parts=1):
        def body(c, carry):
            at = pl.ds(pl.multiple_of(k * piece + c * 128, 128), 128)
            wide[:ROWS, :] = got[:, :, at].astype(jnp.float32).reshape(ROWS, 128)
            for ch in range(16):
                rows[ch * 64:(ch + 1) * 64, at] = (
                    wide[pl.ds(ch, 64, stride=16), :].astype(jnp.bfloat16))
            return carry

        each = piece // 128 // parts
        lax.fori_loop(j * each, (j + 1) * each, body, 0)

    def transform(k, size, first):
        span = stretch(k, size)

        def body(t, carry):
            at = pl.ds(pl.multiple_of(t * 256, 256), 256)
            term = lax.dot_general(
                table[:, span], rows[at, span], NT, preferred_element_type=jnp.float32)
            spec[:, at] = term if first else spec[:, at] + term
            return carry

        lax.fori_loop(0, ROWS // 256, body, 0)

    tell(in_sem.at[0], along_z)
    take_table.wait()
    for i in (0, 1):
        arrived(i)
        reorder(across(i))
    pl.semaphore_wait(in_sem.at[0], 3)
    tell(in_sem.at[1], along_x)
    transform(y_lo * 2, 2, True)
    pl.semaphore_wait(in_sem.at[1], 3)
    tell(in_sem.at[2], along_freq)
    arrived(2)
    reorder(across(2))
    transform(across(2), 1, False)
    for j in range(2):
        arrived(3, j, 2)
        reorder(across(3), j, 2)

    def finish(half):
        span = stretch(across(3))
        re_at = pl.ds(pl.multiple_of(half * 256, 256), 256)
        im_at = pl.ds(pl.multiple_of(BINS + half * 256, 256), 256)

        def body(t, carry):
            at = pl.ds(pl.multiple_of(t * 256, 256), 256)

            def total(part):
                return spec[part, at] + lax.dot_general(
                    table[part, span], rows[at, span], NT, preferred_element_type=jnp.float32)

            re, im = total(re_at), total(im_at)
            spec[re_at, at] = re
            spec[im_at, at] = im
            power = re * re + im * im
            top = power.astype(jnp.bfloat16)
            high[re_at, at] = top
            low[re_at, at] = (power - top.astype(jnp.float32)).astype(jnp.bfloat16)
            return carry

        lax.fori_loop(0, ROWS // 256, body, 0)

    place_ch = pl.ds(pl.multiple_of(chan * 64 + freq * 16, 16), 16)
    place_k = pl.ds(pl.multiple_of(win * 128, 128), 128)

    def white_of(d, h):
        return white.at[pl.ds(d[2] * 128 + (d[0] * 4 + d[1]) * 4 + 2 * h, 2)]

    def send_white(h, d):
        pltpu.make_async_remote_copy(
            src_ref=white_of(d, h),
            dst_ref=a_mat.at[pl.ds(2 * h, 2), place_ch, place_k],
            send_sem=send3, recv_sem=recv3.at[h], device_id=d, device_id_type=MESH,
        ).start()

    def turn(i):
        return y_lo * 3 + (1 - 2 * y_lo) * i

    def send_share(t, h):
        own, *others = spread(t)
        pl.when(t != freq)(lambda: send_white(h, own))
        for d in others:
            send_white(h, d)

    left = lax.broadcasted_iota(jnp.int32, (128, 128), 1) < 64

    def whiten(i, carry):
        t = turn(i)
        first = t * 128
        start = jnp.clip(first - 64, 0, BINS - 256)
        window = pl.ds(pl.multiple_of(start, 64), 256)
        apart = (lax.broadcasted_iota(jnp.int32, (128, 256), 1) + start) - (
            lax.broadcasted_iota(jnp.int32, (128, 256), 0) + first)
        band = jnp.where((apart >= -MARGIN) & (apart <= MARGIN), 1.0, 0.0).astype(jnp.bfloat16)
        smooth = (
            jnp.dot(band, high[window, :], preferred_element_type=jnp.float32)
            + jnp.dot(band, low[window, :], preferred_element_type=jnp.float32)
        ) / (2 * MARGIN + 1)
        scale = lax.rsqrt(smooth + 1e-06)
        re = spec[pl.ds(pl.multiple_of(first, 128), 128), :] * scale
        im = spec[pl.ds(pl.multiple_of(BINS + first, 128), 128), :] * scale
        for c in range(8):
            a, b = re[:, c * 128:(c + 1) * 128], im[:, c * 128:(c + 1) * 128]
            mixed[pl.ds(2 * c, 128, stride=16), :] = jnp.where(left, a, pltpu.roll(b, 64, 1))
            mixed[pl.ds(2 * c + 1, 128, stride=16), :] = jnp.where(left, pltpu.roll(a, 64, 1), b)
        white[pl.ds(pl.multiple_of(first, 128), 128)] = (
            mixed[:128 * 16, :].reshape(128, 16, 128).astype(jnp.bfloat16))
        send_share(t, 0)
        send_share(t, 1)
        return carry

    finish(y_lo)
    pl.semaphore_wait(in_sem.at[2], 3)
    whiten(0, 0)
    finish(1 - y_lo)
    lax.fori_loop(1, BINS // 128, whiten, 0)
    for h in range(2):
        pltpu.make_async_copy(
            white_of((chan, win, freq), h), a_mat.at[pl.ds(2 * h, 2), place_ch, place_k],
            recv3.at[h],
        ).start()

    sign = jnp.where(lax.broadcasted_iota(jnp.int32, (64, 128), 1) < 64, 1.0, -1.0)

    def cross(b, carry):
        def multiply(m, c):
            for h in range(2):
                block = a_mat[b, pl.ds(pl.multiple_of(m * 128 + h * 64, 64), 64), :]
                b_mat[h * 128:h * 128 + 64, :] = block
                for w in range(4):
                    part = block[:, w * 128:(w + 1) * 128].astype(jnp.float32)
                    b_mat[h * 128 + 64:h * 128 + 128, w * 128:(w + 1) * 128] = (
                        pltpu.roll(part, 64, 1) * sign).astype(jnp.bfloat16)
            tile = lax.dot_general(
                a_mat[b], b_mat[...], NT, preferred_element_type=jnp.float32)
            tile = (tile * (1.0 / SEGMENTS)).astype(jnp.bfloat16)
            for h in range(2):
                sums[:, b, m * 2 + h] = tile[:, h * 128:(h + 1) * 128].reshape(32, 16, 128)
            return c

        lax.fori_loop(0, 4, multiply, 0)

        def send_sums(d):
            pltpu.make_async_remote_copy(
                src_ref=sums.at[d[0] * 4 + d[1], b],
                dst_ref=out_ref.at[holder * 4 + b],
                send_sem=send5, recv_sem=recv5, device_id=d, device_id_type=MESH,
            ).start()

        for d in spread(freq)[1:]:
            send_sums(d)
        pltpu.make_async_copy(sums.at[holder, b], out_ref.at[holder * 4 + b], recv5).start()
        return carry

    for h in range(2):
        half = a_mat.at[pl.ds(2 * h, 2)]
        pltpu.make_async_copy(half, half, recv3.at[h]).wait()
        lax.fori_loop(2 * h, 2 * h + 2, cross, 0)

    pltpu.make_async_copy(out_ref, out_ref, recv5).wait()
    pltpu.make_async_copy(got.at[pl.ds(0, 48)], got.at[pl.ds(0, 48)], send1).wait()
    pltpu.make_async_copy(white.at[pl.ds(0, 508)], white.at[pl.ds(0, 508)], send3).wait()
    pltpu.make_async_copy(sums.at[pl.ds(0, 31)], sums.at[pl.ds(0, 31)], send5).wait()


def order_kernel(partner_ref, in_ref, out_ref, wide, out_sem):
    chan = lax.axis_index("chan")
    parts = 8
    size = in_ref.shape[0] // parts

    def body(i, carry):
        span = pl.ds(i * size, size)
        for r in range(8):
            wide[r, span] = in_ref[span, partner_ref[r, chan]].astype(jnp.float32)
            pltpu.make_async_copy(wide.at[r, span], out_ref.at[0, r, span], out_sem).start()
        return carry

    lax.fori_loop(0, parts, body, 0)
    pltpu.make_async_copy(wide, out_ref.at[0], out_sem).wait()


def per_device(samples, partner):
    table = jnp.asarray(tables())
    sums = pl.pallas_call(
        main_kernel,
        out_shape=pltpu.VMEM((128, 8, 16, 128), jnp.bfloat16),
        in_specs=[pl.BlockSpec(memory_space=pl.ANY)] * 2,
        out_specs=pl.BlockSpec(memory_space=pltpu.VMEM),
        scratch_shapes=[
            pltpu.VMEM((2 * BINS, LENGTH), jnp.bfloat16),
            pltpu.VMEM((SEGS, 16, LENGTH), jnp.bfloat16),
            pltpu.VMEM((ROWS + 16, 128), jnp.float32),
            pltpu.VMEM((ROWS, LENGTH), jnp.bfloat16),
            pltpu.VMEM((2 * BINS, ROWS), jnp.float32),
            pltpu.VMEM((BINS, ROWS), jnp.bfloat16),
            pltpu.VMEM((BINS, ROWS), jnp.bfloat16),
            pltpu.VMEM((128 * 16 + 16, 128), jnp.float32),
            pltpu.VMEM((BINS, 16, 128), jnp.bfloat16),
            pltpu.VMEM((4, CHANS, 512), jnp.bfloat16),
            pltpu.VMEM((256, 512), jnp.bfloat16),
            pltpu.VMEM((32, 4, 8, 16, 128), jnp.bfloat16),
        ] + [
            pltpu.SemaphoreType.DMA, pltpu.SemaphoreType.DMA, pltpu.SemaphoreType.DMA((5,))
        ] + [
            pltpu.SemaphoreType.DMA, pltpu.SemaphoreType.DMA((2,)),
            pltpu.SemaphoreType.DMA, pltpu.SemaphoreType.DMA, pltpu.SemaphoreType.REGULAR((3,))],
        compiler_params=pltpu.CompilerParams(
            collective_id=0, has_side_effects=True, vmem_limit_bytes=50 * 2**20),
        name="spectra",
    )(samples, table)
    return pl.pallas_call(
        order_kernel,
        out_shape=jax.ShapeDtypeStruct((1, 8, 128, 16, 128), jnp.float32),
        in_specs=[
            pl.BlockSpec(memory_space=pltpu.SMEM), pl.BlockSpec(memory_space=pltpu.VMEM)],
        out_specs=pl.BlockSpec(memory_space=pl.ANY),
        scratch_shapes=[
            pltpu.VMEM((8, 128, 16, 128), jnp.float32),
            pltpu.SemaphoreType.DMA,
        ],
        compiler_params=pltpu.CompilerParams(vmem_limit_bytes=20 * 2**20),
        name="order",
    )(partner, sums)


def solution(mesh):
    in_specs = (P("win", "chan", "freq"), P())
    out_specs = P("chan", None, "freq", "win", None)
    return jax.shard_map(
        per_device, mesh=mesh, in_specs=in_specs, out_specs=out_specs, check_vma=False
    )
```

```python
import math

import jax
import jax.numpy as jnp
import ml_dtypes
import numpy as np
from jax import lax
from jax.experimental import pallas as pl
from jax.experimental.pallas import tpu as pltpu
from jax.sharding import PartitionSpec as P

MESH = pl.DeviceIdType.MESH
NT = (((1,), (1,)), ((), ()))

LENGTH = 1024
BINS = 512
MARGIN = 64
SEGS = 64
SEGMENTS = 256
BLOCK = 64
CHANS = 512
ROWS = 1024


def tables():
    n = np.arange(LENGTH)[None, :]
    f = np.arange(BINS)[:, None]
    angle = (n * f % LENGTH) * (2.0 * math.pi / LENGTH)
    both = np.concatenate([np.cos(angle), -np.sin(angle)], axis=0) / math.sqrt(LENGTH)
    return both.astype(np.float32).astype(ml_dtypes.bfloat16)


def position():
    chan, win, freq = (lax.axis_index(name) for name in ("chan", "win", "freq"))
    return chan // 4, chan % 4, win, freq // 2, freq % 2


def spread(freq):
    y_hi, x, z, _, _ = position()
    halves = y_hi, 1 - y_hi
    xs = [(x + i) % 4 for i in range(4)]
    zs = [(z + i) % 4 for i in range(4)]
    return [
        (halves[s] * 4 + xs[(i + 2 * s) % 4], zs[(j + 2 * s) % 4], freq)
        for j in range(4) for i in range(4) for s in range(2)
    ]


def main_kernel(
    x_ref, table_ref, out_ref,
    table, got, wide, rows, spec, high, low, mixed, white, a_mat, b_mat, sums,
    table_sem, send1, recv1, send3, recv3, send5, recv5, in_sem,
):
    chan, win, freq = (lax.axis_index(name) for name in ("chan", "win", "freq"))
    holder = chan * 4 + win
    piece = x_ref.shape[2]
    take_table = pltpu.make_async_copy(table_ref, table, table_sem)
    take_table.start()

    barrier = pltpu.get_barrier_semaphore()
    y_hi, x, z, y_lo, core = position()
    along_x = [(y_hi * 4 + (x + i) % 4, win, freq) for i in (1, 2, 3)]
    along_z = [(chan, (z + i) % 4, freq) for i in (1, 2, 3)]
    along_freq = [(chan, win, (freq + i) % 4) for i in (1, 2, 3)]

    def tell(semaphore, devices):
        for d in devices:
            pl.semaphore_signal(semaphore, inc=1, device_id=d, device_id_type=MESH)

    tell(barrier, along_freq + along_x + along_z + [((1 - y_hi) * 4 + x, win, freq)])
    pl.semaphore_wait(barrier, 10)

    def across(i):
        return (y_lo + i // 2) % 2 * 2 + (core + i % 2) % 2

    def stretch(k, size=1):
        return pl.ds(pl.multiple_of(k * piece, size * piece), size * piece)

    def part(k, j, parts):
        size = piece // parts
        return pl.ds(pl.multiple_of(k * piece + j * size, size), size)

    for i, j, parts in ((2, 0, 1), (3, 0, 2), (3, 1, 2), (1, 0, 1)):
        k = across(i)
        pltpu.make_async_remote_copy(
            src_ref=x_ref.at[:, pl.ds(pl.multiple_of(k * 16, 16), 16), part(0, j, parts)],
            dst_ref=got.at[:, :, part(freq, j, parts)],
            send_sem=send1, recv_sem=recv1.at[i + j],
            device_id=(chan, win, k), device_id_type=MESH,
        ).start()

    pltpu.make_async_copy(
        x_ref.at[:, pl.ds(pl.multiple_of(freq * 16, 16), 16), :],
        got.at[:, :, stretch(freq)], recv1.at[0],
    ).start()

    def arrived(i, j=0, parts=1):
        here = got.at[:, :, part(across(i), j, parts)]
        pltpu.make_async_copy(here, here, recv1.at[i + j]).wait()

    def reorder(k, j=0, parts=1):
        def body(c, carry):
            at = pl.ds(pl.multiple_of(k * piece + c * 128, 128), 128)
            wide[:ROWS, :] = got[:, :, at].astype(jnp.float32).reshape(ROWS, 128)
            for ch in range(16):
                rows[ch * 64:(ch + 1) * 64, at] = (
                    wide[pl.ds(ch, 64, stride=16), :].astype(jnp.bfloat16))
            return carry

        each = piece // 128 // parts
        lax.fori_loop(j * each, (j + 1) * each, body, 0)

    def transform(k, size, first):
        span = stretch(k, size)

        def body(t, carry):
            at = pl.ds(pl.multiple_of(t * 256, 256), 256)
            term = lax.dot_general(
                table[:, span], rows[at, span], NT, preferred_element_type=jnp.float32)
            spec[:, at] = term if first else spec[:, at] + term
            return carry

        lax.fori_loop(0, ROWS // 256, body, 0)

    tell(in_sem.at[0], along_z)
    for powers in (high, low):
        powers[192:320, :] = jnp.zeros((128, ROWS), jnp.bfloat16)
    take_table.wait()
    for i in (0, 1):
        arrived(i)
        reorder(across(i))
    pl.semaphore_wait(in_sem.at[0], 3)
    tell(in_sem.at[1], along_x)
    transform(y_lo * 2, 2, True)
    pl.semaphore_wait(in_sem.at[1], 3)
    tell(in_sem.at[2], along_freq)
    arrived(2)
    reorder(across(2))
    transform(across(2), 1, False)
    for j in range(2):
        arrived(3, j, 2)
        reorder(across(3), j, 2)

    def finish(first, size):
        span = stretch(across(3))
        re_at = pl.ds(pl.multiple_of(first, 64), size)
        im_at = pl.ds(pl.multiple_of(BINS + first, 64), size)

        def body(t, carry):
            at = pl.ds(pl.multiple_of(t * 256, 256), 256)

            def total(part):
                return spec[part, at] + lax.dot_general(
                    table[part, span], rows[at, span], NT, preferred_element_type=jnp.float32)

            re, im = total(re_at), total(im_at)
            spec[re_at, at] = re
            spec[im_at, at] = im
            power = re * re + im * im
            top = power.astype(jnp.bfloat16)
            high[re_at, at] = top
            low[re_at, at] = (power - top.astype(jnp.float32)).astype(jnp.bfloat16)
            return carry

        lax.fori_loop(0, ROWS // 256, body, 0)

    place_ch = pl.ds(pl.multiple_of(chan * 64 + freq * 16, 16), 16)
    place_k = pl.ds(pl.multiple_of(win * 128, 128), 128)

    def white_of(d, h):
        return white.at[pl.ds(d[2] * 128 + (d[0] * 4 + d[1]) * 4 + 2 * h, 2)]

    def send_white(h, d):
        pltpu.make_async_remote_copy(
            src_ref=white_of(d, h),
            dst_ref=a_mat.at[pl.ds(2 * h, 2), place_ch, place_k],
            send_sem=send3, recv_sem=recv3.at[h], device_id=d, device_id_type=MESH,
        ).start()

    def turn(i):
        return y_lo * 3 + (1 - 2 * y_lo) * i

    def send_share(t, h):
        own, *others = spread(t)
        pl.when(t != freq)(lambda: send_white(h, own))
        for d in others:
            send_white(h, d)

    left = lax.broadcasted_iota(jnp.int32, (128, 128), 1) < 64

    def whiten(i, carry):
        t = turn(i)
        first = t * 128
        start = jnp.clip(first - 64, 0, BINS - 256)
        window = pl.ds(pl.multiple_of(start, 64), 256)
        apart = (lax.broadcasted_iota(jnp.int32, (128, 256), 1) + start) - (
            lax.broadcasted_iota(jnp.int32, (128, 256), 0) + first)
        band = jnp.where((apart >= -MARGIN) & (apart <= MARGIN), 1.0, 0.0).astype(jnp.bfloat16)
        smooth = (
            jnp.dot(band, high[window, :], preferred_element_type=jnp.float32)
            + jnp.dot(band, low[window, :], preferred_element_type=jnp.float32)
        ) * (1.0 / (2 * MARGIN + 1))
        scale = lax.rsqrt(smooth + 1e-06)
        re = spec[pl.ds(pl.multiple_of(first, 128), 128), :] * scale
        im = spec[pl.ds(pl.multiple_of(BINS + first, 128), 128), :] * scale
        for c in range(8):
            a, b = re[:, c * 128:(c + 1) * 128], im[:, c * 128:(c + 1) * 128]
            mixed[pl.ds(2 * c, 128, stride=16), :] = jnp.where(left, a, pltpu.roll(b, 64, 1))
            mixed[pl.ds(2 * c + 1, 128, stride=16), :] = jnp.where(left, pltpu.roll(a, 64, 1), b)
        white[pl.ds(pl.multiple_of(first, 128), 128)] = (
            mixed[:128 * 16, :].reshape(128, 16, 128).astype(jnp.bfloat16))
        send_share(t, 0)
        send_share(t, 1)
        return carry

    finish(y_lo * 320, 192)
    pl.semaphore_wait(in_sem.at[2], 3)
    whiten(0, 0)
    finish((1 - y_lo) * 192, 320)
    lax.fori_loop(1, BINS // 128, whiten, 0)
    for h in range(2):
        pltpu.make_async_copy(
            white_of((chan, win, freq), h), a_mat.at[pl.ds(2 * h, 2), place_ch, place_k],
            recv3.at[h],
        ).start()

    sign = jnp.where(lax.broadcasted_iota(jnp.int32, (64, 128), 1) < 64, 1.0, -1.0)

    def cross(b, carry):
        def multiply(m, c):
            for h in range(2):
                block = a_mat[b, pl.ds(pl.multiple_of(m * 128 + h * 64, 64), 64), :]
                b_mat[h * 128:h * 128 + 64, :] = block
                for w in range(4):
                    part = block[:, w * 128:(w + 1) * 128].astype(jnp.float32)
                    b_mat[h * 128 + 64:h * 128 + 128, w * 128:(w + 1) * 128] = (
                        pltpu.roll(part, 64, 1) * sign).astype(jnp.bfloat16)
            tile = lax.dot_general(
                a_mat[b], b_mat[...], NT, preferred_element_type=jnp.float32)
            tile = (tile * (1.0 / SEGMENTS)).astype(jnp.bfloat16)
            for h in range(2):
                sums[:, b, m * 2 + h] = tile[:, h * 128:(h + 1) * 128].reshape(32, 16, 128)
            return c

        lax.fori_loop(0, 4, multiply, 0)

        def send_sums(d):
            pltpu.make_async_remote_copy(
                src_ref=sums.at[d[0] * 4 + d[1], b],
                dst_ref=out_ref.at[holder * 4 + b],
                send_sem=send5, recv_sem=recv5, device_id=d, device_id_type=MESH,
            ).start()

        for d in spread(freq)[1:]:
            send_sums(d)
        pltpu.make_async_copy(sums.at[holder, b], out_ref.at[holder * 4 + b], recv5).start()
        return carry

    for h in range(2):
        half = a_mat.at[pl.ds(2 * h, 2)]
        pltpu.make_async_copy(half, half, recv3.at[h]).wait()
        lax.fori_loop(2 * h, 2 * h + 2, cross, 0)

    pltpu.make_async_copy(out_ref, out_ref, recv5).wait()
    pltpu.make_async_copy(got.at[pl.ds(0, 48)], got.at[pl.ds(0, 48)], send1).wait()
    pltpu.make_async_copy(white.at[pl.ds(0, 508)], white.at[pl.ds(0, 508)], send3).wait()
    pltpu.make_async_copy(sums.at[pl.ds(0, 31)], sums.at[pl.ds(0, 31)], send5).wait()


def order_kernel(partner_ref, in_ref, out_ref, wide, out_sem):
    chan = lax.axis_index("chan")
    parts = 8
    size = in_ref.shape[0] // parts

    def body(i, carry):
        span = pl.ds(i * size, size)
        for r in range(8):
            wide[r, span] = in_ref[span, partner_ref[r, chan]].astype(jnp.float32)
            pltpu.make_async_copy(wide.at[r, span], out_ref.at[0, r, span], out_sem).start()
        return carry

    lax.fori_loop(0, parts, body, 0)
    pltpu.make_async_copy(wide, out_ref.at[0], out_sem).wait()


def per_device(samples, partner):
    table = jnp.asarray(tables())
    sums = pl.pallas_call(
        main_kernel,
        out_shape=pltpu.VMEM((128, 8, 16, 128), jnp.bfloat16),
        in_specs=[pl.BlockSpec(memory_space=pl.ANY)] * 2,
        out_specs=pl.BlockSpec(memory_space=pltpu.VMEM),
        scratch_shapes=[
            pltpu.VMEM((2 * BINS, LENGTH), jnp.bfloat16),
            pltpu.VMEM((SEGS, 16, LENGTH), jnp.bfloat16),
            pltpu.VMEM((ROWS + 16, 128), jnp.float32),
            pltpu.VMEM((ROWS, LENGTH), jnp.bfloat16),
            pltpu.VMEM((2 * BINS, ROWS), jnp.float32),
            pltpu.VMEM((BINS, ROWS), jnp.bfloat16),
            pltpu.VMEM((BINS, ROWS), jnp.bfloat16),
            pltpu.VMEM((128 * 16 + 16, 128), jnp.float32),
            pltpu.VMEM((BINS, 16, 128), jnp.bfloat16),
            pltpu.VMEM((4, CHANS, 512), jnp.bfloat16),
            pltpu.VMEM((256, 512), jnp.bfloat16),
            pltpu.VMEM((32, 4, 8, 16, 128), jnp.bfloat16),
        ] + [
            pltpu.SemaphoreType.DMA, pltpu.SemaphoreType.DMA, pltpu.SemaphoreType.DMA((5,))
        ] + [
            pltpu.SemaphoreType.DMA, pltpu.SemaphoreType.DMA((2,)),
            pltpu.SemaphoreType.DMA, pltpu.SemaphoreType.DMA, pltpu.SemaphoreType.REGULAR((3,))],
        compiler_params=pltpu.CompilerParams(
            collective_id=0, has_side_effects=True, vmem_limit_bytes=50 * 2**20),
        name="spectra",
    )(samples, table)
    return pl.pallas_call(
        order_kernel,
        out_shape=jax.ShapeDtypeStruct((1, 8, 128, 16, 128), jnp.float32),
        in_specs=[
            pl.BlockSpec(memory_space=pltpu.SMEM), pl.BlockSpec(memory_space=pltpu.VMEM)],
        out_specs=pl.BlockSpec(memory_space=pl.ANY),
        scratch_shapes=[
            pltpu.VMEM((8, 128, 16, 128), jnp.float32),
            pltpu.SemaphoreType.DMA,
        ],
        compiler_params=pltpu.CompilerParams(vmem_limit_bytes=20 * 2**20),
        name="order",
    )(partner, sums)


def solution(mesh):
    in_specs = (P("win", "chan", "freq"), P())
    out_specs = P("chan", None, "freq", "win", None)
    return jax.shard_map(
        per_device, mesh=mesh, in_specs=in_specs, out_specs=out_specs, check_vma=False
    )
```

```python
import math

import jax
import jax.numpy as jnp
import ml_dtypes
import numpy as np
from jax import lax
from jax.experimental import pallas as pl
from jax.experimental.pallas import tpu as pltpu
from jax.sharding import PartitionSpec as P

MESH = pl.DeviceIdType.MESH
NT = (((1,), (1,)), ((), ()))

LENGTH = 1024
BINS = 512
MARGIN = 64
SEGS = 64
SEGMENTS = 256
BLOCK = 64
CHANS = 512
ROWS = 1024


def tables():
    n = np.arange(LENGTH)[None, :]
    f = np.arange(BINS)[:, None]
    angle = (n * f % LENGTH) * (2.0 * math.pi / LENGTH)
    both = np.concatenate([np.cos(angle), -np.sin(angle)], axis=0) / math.sqrt(LENGTH)
    return both.astype(np.float32).astype(ml_dtypes.bfloat16)


def position():
    chan, win, freq = (lax.axis_index(name) for name in ("chan", "win", "freq"))
    return chan // 4, chan % 4, win, freq // 2, freq % 2


IN_TURN = [(i, j) for j in range(4) for i in range(4)]
MIXED = [(0, 0)] + [(2, 2), (0, 1), (3, 1), (1, 3), (3, 2), (0, 2), (1, 2), (1, 1), (3, 0), (2, 1), (0, 3), (2, 0), (1, 0), (3, 3), (2, 3)]


def spread(freq, order=IN_TURN):
    y_hi, x, z, _, _ = position()
    halves = y_hi, 1 - y_hi
    xs = [(x + i) % 4 for i in range(4)]
    zs = [(z + i) % 4 for i in range(4)]
    return [
        (halves[s] * 4 + xs[(i + 2 * s) % 4], zs[(j + 2 * s) % 4], freq)
        for i, j in order for s in range(2)
    ]


def main_kernel(
    x_ref, table_ref, out_ref,
    table, got, wide, rows, spec, high, low, mixed, white, a_mat, b_mat, sums,
    table_sem, send1, recv1, send3, recv3, send5, recv5, in_sem,
):
    chan, win, freq = (lax.axis_index(name) for name in ("chan", "win", "freq"))
    holder = chan * 4 + win
    piece = x_ref.shape[2]
    take_table = pltpu.make_async_copy(table_ref, table, table_sem)
    take_table.start()

    barrier = pltpu.get_barrier_semaphore()
    y_hi, x, z, y_lo, core = position()
    along_x = [(y_hi * 4 + (x + i) % 4, win, freq) for i in (1, 2, 3)]
    along_z = [(chan, (z + i) % 4, freq) for i in (1, 2, 3)]
    along_freq = [(chan, win, (freq + i) % 4) for i in (1, 2, 3)]

    def tell(semaphore, devices):
        for d in devices:
            pl.semaphore_signal(semaphore, inc=1, device_id=d, device_id_type=MESH)

    tell(barrier, along_freq + along_x + along_z + [((1 - y_hi) * 4 + x, win, freq)])
    pl.semaphore_wait(barrier, 10)

    def across(i):
        return (y_lo + i // 2) % 2 * 2 + (core + i % 2) % 2

    def stretch(k, size=1):
        return pl.ds(pl.multiple_of(k * piece, size * piece), size * piece)

    def part(k, j, parts):
        size = piece // parts
        return pl.ds(pl.multiple_of(k * piece + j * size, size), size)

    for i, j, parts in ((2, 0, 1), (3, 0, 2), (3, 1, 2), (1, 0, 1)):
        k = across(i)
        pltpu.make_async_remote_copy(
            src_ref=x_ref.at[:, pl.ds(pl.multiple_of(k * 16, 16), 16), part(0, j, parts)],
            dst_ref=got.at[:, :, part(freq, j, parts)],
            send_sem=send1, recv_sem=recv1.at[i + j],
            device_id=(chan, win, k), device_id_type=MESH,
        ).start()

    pltpu.make_async_copy(
        x_ref.at[:, pl.ds(pl.multiple_of(freq * 16, 16), 16), :],
        got.at[:, :, stretch(freq)], recv1.at[0],
    ).start()

    def arrived(i, j=0, parts=1):
        here = got.at[:, :, part(across(i), j, parts)]
        pltpu.make_async_copy(here, here, recv1.at[i + j]).wait()

    def reorder(k, j=0, parts=1):
        def body(c, carry):
            at = pl.ds(pl.multiple_of(k * piece + c * 128, 128), 128)
            wide[:ROWS, :] = got[:, :, at].astype(jnp.float32).reshape(ROWS, 128)
            for ch in range(16):
                rows[ch * 64:(ch + 1) * 64, at] = (
                    wide[pl.ds(ch, 64, stride=16), :].astype(jnp.bfloat16))
            return carry

        each = piece // 128 // parts
        lax.fori_loop(j * each, (j + 1) * each, body, 0)

    def transform(k, size, first):
        span = stretch(k, size)

        def body(t, carry):
            at = pl.ds(pl.multiple_of(t * 256, 256), 256)
            term = lax.dot_general(
                table[:, span], rows[at, span], NT, preferred_element_type=jnp.float32)
            spec[:, at] = term if first else spec[:, at] + term
            return carry

        lax.fori_loop(0, ROWS // 256, body, 0)

    tell(in_sem.at[0], along_z)
    take_table.wait()
    for i in (0, 1):
        arrived(i)
        reorder(across(i))
    pl.semaphore_wait(in_sem.at[0], 3)
    tell(in_sem.at[1], along_x)
    transform(y_lo * 2, 2, True)
    pl.semaphore_wait(in_sem.at[1], 3)
    tell(in_sem.at[2], along_freq)
    arrived(2)
    reorder(across(2))
    transform(across(2), 1, False)
    for j in range(2):
        arrived(3, j, 2)
        reorder(across(3), j, 2)

    def finish(half):
        span = stretch(across(3))
        re_at = pl.ds(pl.multiple_of(half * 256, 256), 256)
        im_at = pl.ds(pl.multiple_of(BINS + half * 256, 256), 256)

        def body(t, carry):
            at = pl.ds(pl.multiple_of(t * 256, 256), 256)

            def total(part):
                return spec[part, at] + lax.dot_general(
                    table[part, span], rows[at, span], NT, preferred_element_type=jnp.float32)

            re, im = total(re_at), total(im_at)
            spec[re_at, at] = re
            spec[im_at, at] = im
            power = re * re + im * im
            top = power.astype(jnp.bfloat16)
            high[re_at, at] = top
            low[re_at, at] = (power - top.astype(jnp.float32)).astype(jnp.bfloat16)
            return carry

        lax.fori_loop(0, ROWS // 256, body, 0)

    place_ch = pl.ds(pl.multiple_of(chan * 64 + freq * 16, 16), 16)
    place_k = pl.ds(pl.multiple_of(win * 128, 128), 128)

    def white_of(d, h):
        return white.at[pl.ds(d[2] * 128 + (d[0] * 4 + d[1]) * 4 + 2 * h, 2)]

    def send_white(h, d):
        pltpu.make_async_remote_copy(
            src_ref=white_of(d, h),
            dst_ref=a_mat.at[pl.ds(2 * h, 2), place_ch, place_k],
            send_sem=send3, recv_sem=recv3.at[h], device_id=d, device_id_type=MESH,
        ).start()

    def turn(i):
        return y_lo * 3 + (1 - 2 * y_lo) * i

    def send_share(t, h):
        own, *others = spread(t)
        pl.when(t != freq)(lambda: send_white(h, own))
        for d in others:
            send_white(h, d)

    left = lax.broadcasted_iota(jnp.int32, (128, 128), 1) < 64

    def whiten(i, carry):
        t = turn(i)
        first = t * 128
        start = jnp.clip(first - 64, 0, BINS - 256)
        window = pl.ds(pl.multiple_of(start, 64), 256)
        apart = (lax.broadcasted_iota(jnp.int32, (128, 256), 1) + start) - (
            lax.broadcasted_iota(jnp.int32, (128, 256), 0) + first)
        band = jnp.where((apart >= -MARGIN) & (apart <= MARGIN), 1.0, 0.0).astype(jnp.bfloat16)
        smooth = (
            jnp.dot(band, high[window, :], preferred_element_type=jnp.float32)
            + jnp.dot(band, low[window, :], preferred_element_type=jnp.float32)
        ) / (2 * MARGIN + 1)
        scale = lax.rsqrt(smooth + 1e-06)
        re = spec[pl.ds(pl.multiple_of(first, 128), 128), :] * scale
        im = spec[pl.ds(pl.multiple_of(BINS + first, 128), 128), :] * scale
        for c in range(8):
            a, b = re[:, c * 128:(c + 1) * 128], im[:, c * 128:(c + 1) * 128]
            mixed[pl.ds(2 * c, 128, stride=16), :] = jnp.where(left, a, pltpu.roll(b, 64, 1))
            mixed[pl.ds(2 * c + 1, 128, stride=16), :] = jnp.where(left, pltpu.roll(a, 64, 1), b)
        white[pl.ds(pl.multiple_of(first, 128), 128)] = (
            mixed[:128 * 16, :].reshape(128, 16, 128).astype(jnp.bfloat16))
        send_share(t, 0)
        send_share(t, 1)
        return carry

    finish(y_lo)
    pl.semaphore_wait(in_sem.at[2], 3)
    whiten(0, 0)
    finish(1 - y_lo)
    lax.fori_loop(1, BINS // 128, whiten, 0)
    for h in range(2):
        pltpu.make_async_copy(
            white_of((chan, win, freq), h), a_mat.at[pl.ds(2 * h, 2), place_ch, place_k],
            recv3.at[h],
        ).start()

    sign = jnp.where(lax.broadcasted_iota(jnp.int32, (64, 128), 1) < 64, 1.0, -1.0)

    def cross(b, carry):
        def multiply(m, c):
            for h in range(2):
                block = a_mat[b, pl.ds(pl.multiple_of(m * 128 + h * 64, 64), 64), :]
                b_mat[h * 128:h * 128 + 64, :] = block
                for w in range(4):
                    part = block[:, w * 128:(w + 1) * 128].astype(jnp.float32)
                    b_mat[h * 128 + 64:h * 128 + 128, w * 128:(w + 1) * 128] = (
                        pltpu.roll(part, 64, 1) * sign).astype(jnp.bfloat16)
            tile = lax.dot_general(
                a_mat[b], b_mat[...], NT, preferred_element_type=jnp.float32)
            tile = (tile * (1.0 / SEGMENTS)).astype(jnp.bfloat16)
            for h in range(2):
                sums[:, b, m * 2 + h] = tile[:, h * 128:(h + 1) * 128].reshape(32, 16, 128)
            return c

        lax.fori_loop(0, 4, multiply, 0)

        def send_sums(d):
            pltpu.make_async_remote_copy(
                src_ref=sums.at[d[0] * 4 + d[1], b],
                dst_ref=out_ref.at[holder * 4 + b],
                send_sem=send5, recv_sem=recv5, device_id=d, device_id_type=MESH,
            ).start()

        for d in spread(freq, MIXED)[1:]:
            send_sums(d)
        pltpu.make_async_copy(sums.at[holder, b], out_ref.at[holder * 4 + b], recv5).start()
        return carry

    for h in range(2):
        half = a_mat.at[pl.ds(2 * h, 2)]
        pltpu.make_async_copy(half, half, recv3.at[h]).wait()
        lax.fori_loop(2 * h, 2 * h + 2, cross, 0)

    pltpu.make_async_copy(out_ref, out_ref, recv5).wait()
    pltpu.make_async_copy(got.at[pl.ds(0, 48)], got.at[pl.ds(0, 48)], send1).wait()
    pltpu.make_async_copy(white.at[pl.ds(0, 508)], white.at[pl.ds(0, 508)], send3).wait()
    pltpu.make_async_copy(sums.at[pl.ds(0, 31)], sums.at[pl.ds(0, 31)], send5).wait()


def order_kernel(partner_ref, in_ref, out_ref, wide, out_sem):
    chan = lax.axis_index("chan")
    parts = 8
    size = in_ref.shape[0] // parts

    def body(i, carry):
        span = pl.ds(i * size, size)
        for r in range(8):
            wide[r, span] = in_ref[span, partner_ref[r, chan]].astype(jnp.float32)
            pltpu.make_async_copy(wide.at[r, span], out_ref.at[0, r, span], out_sem).start()
        return carry

    lax.fori_loop(0, parts, body, 0)
    pltpu.make_async_copy(wide, out_ref.at[0], out_sem).wait()


def per_device(samples, partner):
    table = jnp.asarray(tables())
    sums = pl.pallas_call(
        main_kernel,
        out_shape=pltpu.VMEM((128, 8, 16, 128), jnp.bfloat16),
        in_specs=[pl.BlockSpec(memory_space=pl.ANY)] * 2,
        out_specs=pl.BlockSpec(memory_space=pltpu.VMEM),
        scratch_shapes=[
            pltpu.VMEM((2 * BINS, LENGTH), jnp.bfloat16),
            pltpu.VMEM((SEGS, 16, LENGTH), jnp.bfloat16),
            pltpu.VMEM((ROWS + 16, 128), jnp.float32),
            pltpu.VMEM((ROWS, LENGTH), jnp.bfloat16),
            pltpu.VMEM((2 * BINS, ROWS), jnp.float32),
            pltpu.VMEM((BINS, ROWS), jnp.bfloat16),
            pltpu.VMEM((BINS, ROWS), jnp.bfloat16),
            pltpu.VMEM((128 * 16 + 16, 128), jnp.float32),
            pltpu.VMEM((BINS, 16, 128), jnp.bfloat16),
            pltpu.VMEM((4, CHANS, 512), jnp.bfloat16),
            pltpu.VMEM((256, 512), jnp.bfloat16),
            pltpu.VMEM((32, 4, 8, 16, 128), jnp.bfloat16),
        ] + [
            pltpu.SemaphoreType.DMA, pltpu.SemaphoreType.DMA, pltpu.SemaphoreType.DMA((5,))
        ] + [
            pltpu.SemaphoreType.DMA, pltpu.SemaphoreType.DMA((2,)),
            pltpu.SemaphoreType.DMA, pltpu.SemaphoreType.DMA, pltpu.SemaphoreType.REGULAR((3,))],
        compiler_params=pltpu.CompilerParams(
            collective_id=0, has_side_effects=True, vmem_limit_bytes=50 * 2**20),
        name="spectra",
    )(samples, table)
    return pl.pallas_call(
        order_kernel,
        out_shape=jax.ShapeDtypeStruct((1, 8, 128, 16, 128), jnp.float32),
        in_specs=[
            pl.BlockSpec(memory_space=pltpu.SMEM), pl.BlockSpec(memory_space=pltpu.VMEM)],
        out_specs=pl.BlockSpec(memory_space=pl.ANY),
        scratch_shapes=[
            pltpu.VMEM((8, 128, 16, 128), jnp.float32),
            pltpu.SemaphoreType.DMA,
        ],
        compiler_params=pltpu.CompilerParams(vmem_limit_bytes=20 * 2**20),
        name="order",
    )(partner, sums)


def solution(mesh):
    in_specs = (P("win", "chan", "freq"), P())
    out_specs = P("chan", None, "freq", "win", None)
    return jax.shard_map(
        per_device, mesh=mesh, in_specs=in_specs, out_specs=out_specs, check_vma=False
    )
```
